32 devices in a mesh: rep: 8 (over z, x), tp: 4 (over y, core).
Axes of the slice: x: 2, y: 2, z: 4, core: 2. Of those that a mesh axis runs over, the one named last changes fastest.
Arguments:
- hidden: bfloat16 [8192, 4096], P('rep'), may hold values from -6 to 6
- norm_gain: bfloat16 [4096], replicated, may hold values from 0.099609375 to 1.8984375
- w_query: bfloat16 [4096, 4096], P('rep', 'tp'), may hold values from -0.09375 to 0.09375
- w_keyval: bfloat16 [4096, 1024], P('rep', 'tp'), may hold values from -0.09375 to 0.09375
- w_output: bfloat16 [4096, 4096], P('tp', 'rep'), may hold values from -0.09375 to 0.09375
- cache: bfloat16 [16384, 1024], P('rep'), may hold values from -190 to 190
- lengths: int32 [8, 4], P('rep'), may hold values from 1 to 640, 1024 in all within a row
- prefix: int32 [32], P('rep'), may hold values from 1 to 512, 8192 in all
- out_gain: bfloat16 [4096], replicated, may hold values from 0.099609375 to 1.8984375
Outputs:
- resid: bfloat16 [8192, 4096], P('rep', 'tp')
- normed: bfloat16 [8192, 4096], P('rep', 'tp')
The draws below stay inside these ranges and needn't reach their ends.
Inputs may be any that keep to these rules, and one draw needn't show every extreme that they name: `lengths`: each row sums to 1024, and some request has 640 new tokens. All prefixes sum to 8192, and some request has a prefix of 512.
All inputs are finite; a program needn't handle non-finite values. No bound on the sum of `prefix` on one device may be relied on, other than what follows from the above.
Results may differ from the reference program's by a relative error of at most 0.0095.
Values may be sent and summed in bfloat16 or wider, within the bound.
No kernel may reach another device: no remote copies, remote signals or barrier semaphores. Data moves between devices by JAX's collectives and lax.ppermute only.
A program may use at most 128 MiB of HBM per device.

```python
import math
import jax
import jax.numpy as jnp
import numpy as np
from jax import lax

D = 4096
H = 32
KV = 4
HD = 128
TOK_REP = 1024
REQ_REP = 4
PREF_MAX = 512
MOST_LEN = 640
REPS = 8
REQUESTS = 32
TOKENS = 8192
PREF_TOTAL = 8192
N_REP = 8
N_TP = 4


def draw_cache(key, part):
    key_noise, key_sign, key_strength, key_head = jax.random.split(jax.random.fold_in(key, 11), 4)
    shape = (REQUESTS, PREF_MAX, KV, 2, HD)
    noise = jnp.clip(jax.random.normal(key_noise, shape, jnp.float32), -6.0, 6.0)
    strength = jax.random.uniform(key_strength, (REQUESTS,), jnp.float32, 60.0, 160.0)
    sign_pattern = jnp.where(jax.random.bernoulli(key_sign, 0.5, (REQUESTS, HD)), 1.0, -1.0)
    sink_head = jax.random.randint(key_head, (REQUESTS,), 0, KV)
    slot_ids = jnp.arange(PREF_MAX, dtype=jnp.int32)
    head_ids = jnp.arange(KV, dtype=jnp.int32)
    stretch = jnp.where(slot_ids == 0, 1.0, 1.012).astype(jnp.float32)
    sink = strength[:, None, None, None] * stretch[None, :, None, None] * sign_pattern[:, None, None, :]
    chosen = (slot_ids[None, :, None] < 2) & (head_ids[None, None, :] == sink_head[:, None, None])
    key_part = jnp.where(chosen[..., None], sink, noise[:, :, :, 0, :])
    stacked = jnp.stack([key_part, noise[:, :, :, 1, :]], axis=3)
    return stacked.reshape(REQUESTS * PREF_MAX, 2 * KV * HD).astype(jnp.bfloat16)


def levels(rng, shape, cuts, smallest, high):
    def one(dim, blocks):
        heights = jax.random.uniform(jax.random.fold_in(jax.random.fold_in(rng, 6), dim), (blocks,), jnp.float32, smallest / len(cuts), high / len(cuts))
        return jnp.repeat(jnp.exp(heights), shape[dim] // blocks).reshape((-1,) + (1,) * (len(shape) - dim - 1))

    factor_of = one(*cuts[0])
    for cut in cuts[1:]:
        factor_of = factor_of * one(*cut)
    return factor_of


def split_up(number_of, total, bound, lean):
    portions = [(1 << 20) // math.isqrt(grade ** lean) + 1 for grade in range(2, number_of + 1)]
    spare, counts = total - bound - (number_of - 1), [1] * (number_of - 1)
    while spare > 0:
        candidates = [i for i in range(number_of - 1) if counts[i] < bound]
        mass, budget = sum([portions[i] for i in candidates]), spare
        for i in candidates:
            addition = min(bound - counts[i], max(1, budget * portions[i] // mass), spare)
            counts[i] = counts[i] + addition
            spare = spare - addition
    return np.array([bound] + counts)


def uneven(rng, amount, total, reach, slope):
    if amount == 2:
        one = jax.random.randint(rng, (), max(1, total - reach), min(reach, total - 1) + 1)
        return jnp.stack([one, total - one])
    tallies = jnp.asarray(split_up(amount, total, reach, slope), jnp.int32)
    twos = (amount - 1) // 2
    donor, receiver = tallies[1:1 + 2 * twos:2], tallies[2:2 + 2 * twos:2]
    slack = jnp.minimum(donor - 1, reach - receiver)
    moved = jax.random.randint(jax.random.fold_in(rng, 1), (twos,), 0, 1 << 20) % (slack + 1)
    tallies = tallies.at[1:1 + 2 * twos:2].set(donor - moved).at[2:2 + 2 * twos:2].set(receiver + moved)
    return tallies[jax.random.permutation(jax.random.fold_in(rng, 2), amount)]


def centred(stream_key, shape, scale, reach, shards=(), kind=jnp.bfloat16):
    result = jax.random.normal(stream_key, shape, jnp.float32) * scale
    if len(shards) > 0:
        result = levels(stream_key, shape, shards, -0.22, 0.18) * result
    return jnp.clip(result, min=-reach, max=reach).astype(kind)


def setup_inputs(seed: int = 0) -> dict:
    seeds = jax.random.split(jax.random.key(seed), 10)
    return {
        "hidden": centred(seeds[0], (TOKENS, D), 1.0, 6.0, ((0, 8),)),
        "norm_gain": jnp.clip(1.0 + 0.18 * jax.random.normal(seeds[1], (D,), jnp.float32), 0.099609375, 1.8984375).astype(jnp.bfloat16),
        "w_query": centred(seeds[2], (D, H * HD), D ** -0.5, 0.09375, ((0, 8), (1, 4))),
        "w_keyval": centred(seeds[3], (D, 2 * KV * HD), D ** -0.5, 0.09375, ((0, 8), (1, 4))),
        "w_output": centred(seeds[4], (H * HD, D), (H * HD) ** -0.5, 0.09375, ((0, 4), (1, 8))),
        "cache": draw_cache(jax.random.fold_in(seeds[9], 71), 0),
        "lengths": jax.vmap(lambda own: uneven(own, REQ_REP, TOK_REP, MOST_LEN, 1))(jax.random.split(seeds[6], REPS)).reshape((REPS, REQ_REP)).astype(jnp.int32),
        "prefix": uneven(seeds[7], REQUESTS, PREF_TOTAL, PREF_MAX, 2).astype(jnp.int32),
        "out_gain": jnp.clip(1.0 + 0.18 * jax.random.normal(seeds[8], (D,), jnp.float32), 0.099609375, 1.8984375).astype(jnp.bfloat16),
    }


norm_eps = 1e-05
rope_base = 5000000.0
masked_score = -1e+30

def rms_scale(values, weights):
    meansq = lax.optimization_barrier(jnp.mean(values * values, axis=-1, keepdims=True))
    return values * lax.rsqrt(meansq + norm_eps) * weights

def rotate(values, positions):
    half_dim = values.shape[-1] // 2
    freqs = rope_base ** (-(jnp.arange(half_dim, dtype=jnp.float32) * 2.0 / values.shape[-1]))
    angles = positions.astype(jnp.float32)[:, None] * freqs[None, :]
    cosine = jnp.cos(angles)[:, None, :]
    sine = jnp.sin(angles)[:, None, :]
    first = values[..., :half_dim]
    second = values[..., half_dim:]
    return jnp.concatenate([first * cosine - second * sine, second * cosine + first * sine], axis=-1)

def request_layout(lens, prefs, count):
    token_ids = jnp.arange(count, dtype=jnp.int32)
    ends = jnp.cumsum(lens).astype(jnp.int32)
    starts = ends - lens
    segment = lax.optimization_barrier(jnp.sum((token_ids[:, None] >= ends[None, :]).astype(jnp.int32), axis=1))
    onehot = segment[:, None] == jnp.arange(lens.shape[0], dtype=jnp.int32)[None, :]
    offset = token_ids - lax.optimization_barrier(jnp.sum(jnp.where(onehot, starts[None, :], 0), axis=1))
    position = offset + lax.optimization_barrier(jnp.sum(jnp.where(onehot, prefs[None, :], 0), axis=1))
    return (token_ids, segment, position)

def reference(hidden, norm_gain, w_query, w_keyval, w_output, cache, lengths, prefix, out_gain):
    group_size = H // KV
    blocks_hidden = hidden.reshape(N_REP, TOK_REP, D)
    blocks_pref = prefix.reshape(N_REP, REQ_REP)
    blocks_cache = cache.reshape(N_REP, REQ_REP * PREF_MAX, 2 * KV * HD)
    wo_groups = w_output.reshape(N_TP, H * HD // N_TP, D).astype(jnp.float32)

    def one_group(items):
        block, lens, prefs, cached = items
        normed_in = rms_scale(block.astype(jnp.float32), norm_gain.astype(jnp.float32)).astype(jnp.bfloat16)
        queries = jnp.dot(normed_in, w_query, preferred_element_type=jnp.float32).reshape(TOK_REP, H, HD)
        fresh = jnp.dot(normed_in, w_keyval, preferred_element_type=jnp.float32).astype(jnp.bfloat16)
        fresh = fresh.reshape(TOK_REP, 2, HD, KV).transpose(0, 3, 1, 2)
        token_ids, segment, position = request_layout(lens, prefs, TOK_REP)
        queries = rotate(queries, position).astype(jnp.bfloat16)
        new_keys = rotate(fresh[:, :, 0, :].astype(jnp.float32), position).astype(jnp.bfloat16)
        new_vals = fresh[:, :, 1, :]
        stored = cached.reshape(REQ_REP * PREF_MAX, KV, 2, HD)
        slot_ids = jnp.arange(REQ_REP * PREF_MAX, dtype=jnp.int32)
        slot_req = slot_ids // PREF_MAX
        slot_pos = slot_ids % PREF_MAX
        req_ids = jnp.arange(REQ_REP, dtype=jnp.int32)
        slot_len = lax.optimization_barrier(jnp.sum(jnp.where(slot_req[:, None] == req_ids[None, :], prefs[None, :], 0), axis=1))
        cache_ok = (segment[:, None] == slot_req[None, :]) & (slot_pos < slot_len)[None, :]
        own_ok = (segment[:, None] == segment[None, :]) & (token_ids[None, :] <= token_ids[:, None])
        allowed = jnp.concatenate([cache_ok, own_ok], axis=1)
        all_keys = jnp.concatenate([stored[:, :, 0, :], new_keys], axis=0).astype(jnp.float32)
        all_vals = jnp.concatenate([stored[:, :, 1, :], new_vals], axis=0).astype(jnp.float32)
        grouped = queries.reshape(TOK_REP, KV, group_size, HD).astype(jnp.float32)
        scores = jnp.einsum('tkgd,skd->kgts', grouped, all_keys) * HD ** (-0.5)
        scores = jnp.where(allowed[None, None], scores, masked_score)
        peak = lax.optimization_barrier(jnp.max(scores, axis=-1, keepdims=True))
        expo = jnp.where(allowed[None, None], jnp.exp(scores - peak), 0.0)
        total = lax.optimization_barrier(jnp.sum(expo, axis=-1))
        rounded = lax.optimization_barrier(expo.astype(jnp.bfloat16)).astype(jnp.float32)
        summed = jnp.einsum('kgts,skd->kgtd', rounded, all_vals)
        attended = (summed / total[..., None]).transpose(2, 0, 1, 3).reshape(TOK_REP, H * HD)
        attended = attended.astype(jnp.bfloat16)
        groups = attended.reshape(TOK_REP, N_TP, H * HD // N_TP).astype(jnp.float32)
        parts = jnp.einsum('tnc,ncd->ntd', groups, wo_groups)
        parts = lax.optimization_barrier(parts.astype(jnp.bfloat16)).astype(jnp.float32)
        proj = lax.optimization_barrier(jnp.sum(parts, axis=0))
        resid = (block.astype(jnp.float32) + proj).astype(jnp.bfloat16)
        normed = rms_scale(resid.astype(jnp.float32), out_gain.astype(jnp.float32)).astype(jnp.bfloat16)
        return (resid, normed)
    resid, normed = lax.map(one_group, (blocks_hidden, lengths, blocks_pref, blocks_cache))
    return (resid.reshape(TOKENS, D), normed.reshape(TOKENS, D))
```

```python
import functools

import jax
import jax.numpy as jnp
import numpy as np
from jax import lax
from jax.experimental import pallas as pl
from jax.experimental.pallas import tpu as pltpu
from jax.sharding import PartitionSpec as P

H = 32
KV = 4
HD = 128
REQ_REP = 4
PREF_MAX = 512

norm_eps = 1e-05
rope_base = 5000000.0
masked_score = -1e30
lowest_peak = -1e25

VMEM_LIMIT = 56 * 1024 * 1024


def rms_scale(values, weights):
    meansq = jnp.mean(values * values, axis=-1, keepdims=True)
    return values * lax.rsqrt(meansq + norm_eps) * weights


def ring_order(count):
    return list(range(0, count, 2)) + list(range(count - 1, 0, -2))


def bit_reverse(value, bits):
    return sum(((value >> b) & 1) << (bits - 1 - b) for b in range(bits))


def tables(n_rep, n_tp):
    order = ring_order(n_rep)
    place = [order.index(r) for r in range(n_rep)]
    halves = 2 * n_rep // n_tp
    source = np.zeros((n_rep, 2 * n_rep), np.int32)
    piece = np.zeros((n_rep, n_tp, halves), np.int32)
    column = np.zeros((n_rep, n_tp, halves), np.int32)
    last = [0] * halves
    for r in range(n_rep):
        seen = [0] * n_tp
        for k in range(n_rep):
            for h, src in ((0, order[(place[r] - k) % n_rep]), (1, order[(place[r] + k) % n_rep])):
                source[r, 2 * k + h] = src * 2 + h
                dest = src * n_tp // n_rep
                s = seen[dest]
                seen[dest] += 1
                piece[r, dest, s] = 2 * k + h
                column[r, dest, s] = src * 2 + h - dest * halves
                last[s] = max(last[s], k)
    return order, source, piece, column, last


def rope_tables(position):
    half = HD // 2
    freqs = rope_base ** (-(jnp.arange(half, dtype=jnp.float32) * 2.0 / HD))
    angles = position.astype(jnp.float32)[:, None] * freqs[None, :]
    cosine, sine = jnp.cos(angles), jnp.sin(angles)
    return jnp.concatenate([cosine, cosine], 1), jnp.concatenate([-sine, sine], 1)


def request_position(lens, prefs, count):
    token_ids = jnp.arange(count, dtype=jnp.int32)
    ends = jnp.cumsum(lens)
    starts = ends - lens
    segment = jnp.sum((token_ids[:, None] >= ends[None, :]).astype(jnp.int32), axis=1)
    onehot = segment[:, None] == jnp.arange(lens.shape[0], dtype=jnp.int32)[None, :]
    shift = jnp.sum(jnp.where(onehot, (prefs - starts)[None, :], 0), axis=1)
    return token_ids + shift, starts, ends


def project_kernel(index, x_ref, *rest, count, depth, final, has_acc, heads):
    pieces, rest = rest[:count], rest[count:]
    if has_acc:
        acc_ref, rest = rest[0], rest[1:]
    if final:
        cos_ref, sin_ref, q_ref, k_ref, v_ref, held, sems = rest
    else:
        out_ref, held, sems = rest

    @pl.when(pl.program_id(0) == 0)
    def _():
        copies = [
            pltpu.make_async_copy(pieces[i], held.at[pl.ds(i * depth, depth)], sems.at[i])
            for i in range(count)
        ]
        for copy in copies:
            copy.start()
        for copy in copies:
            copy.wait()

    x = jnp.concatenate(
        [
            x_ref[:, pl.ds(pl.multiple_of(index[i] * depth, depth), depth)]
            for i in range(count)
        ],
        axis=1,
    )
    total = jnp.dot(x, held[...], preferred_element_type=jnp.float32)
    if has_acc:
        total = total + acc_ref[...]
    if not final:
        out_ref[...] = total
        return
    cosine, sine = cos_ref[...], sin_ref[...]

    def rotate(u):
        return (u * cosine + pltpu.roll(u, HD // 2, 1) * sine).astype(jnp.bfloat16)

    for h in range(heads):
        q_ref[:, h * HD : (h + 1) * HD] = rotate(total[:, h * HD : (h + 1) * HD])
    key = total[:, heads * HD : (heads + 1) * HD]
    k_ref[...] = rotate(key.astype(jnp.bfloat16).astype(jnp.float32))
    v_ref[...] = total[:, (heads + 1) * HD :].astype(jnp.bfloat16)


def project(index, x, pieces, acc=None, rope=None, tile=256):
    rows, model = x.shape
    depth, width = pieces[0].shape
    count = len(pieces)
    heads = width // HD - 2
    final = rope is not None
    row_block = lambda w: pl.BlockSpec((tile, w), lambda i, *_: (i, 0))
    in_specs = [row_block(model)] + [pl.BlockSpec(memory_space=pl.ANY)] * count
    args = [x] + list(pieces)
    if acc is not None:
        in_specs.append(row_block(width))
        args.append(acc)
    if final:
        in_specs += [row_block(HD)] * 2
        args += list(rope)
        out_shape = [
            jax.ShapeDtypeStruct((rows, heads * HD), jnp.bfloat16),
            jax.ShapeDtypeStruct((rows, HD), jnp.bfloat16),
            jax.ShapeDtypeStruct((rows, HD), jnp.bfloat16),
        ]
        out_specs = [row_block(heads * HD), row_block(HD), row_block(HD)]
    else:
        out_shape = jax.ShapeDtypeStruct((rows, width), jnp.float32)
        out_specs = row_block(width)
    return pl.pallas_call(
        functools.partial(
            project_kernel,
            count=count,
            depth=depth,
            final=final,
            has_acc=acc is not None,
            heads=heads,
        ),
        out_shape=out_shape,
        grid_spec=pltpu.PrefetchScalarGridSpec(
            num_scalar_prefetch=1,
            grid=(rows // tile,),
            in_specs=in_specs,
            out_specs=out_specs,
            scratch_shapes=[
                pltpu.VMEM((count * depth, width), jnp.bfloat16),
                pltpu.SemaphoreType.DMA((count,)),
            ],
        ),
        compiler_params=pltpu.CompilerParams(vmem_limit_bytes=VMEM_LIMIT),
        cost_estimate=pl.CostEstimate(
            flops=2 * rows * count * depth * width,
            bytes_accessed=rows * model * 2 + count * depth * width * 2 + rows * width * 4,
            transcendentals=0,
        ),
        name="project",
    )(index, *args)


def attend_kernel(
    scal, q_ref, k_ref, v_ref, c_ref, o_ref, m_ref, l_ref, acc_ref, *, first, heads, tq, tc
):
    base = first + pl.program_id(0) * tq
    rows = heads * tq
    q = jnp.concatenate([q_ref[:, h * HD : (h + 1) * HD] for h in range(heads)], axis=0)
    m_ref[...] = jnp.full((rows, HD), lowest_peak, jnp.float32)
    l_ref[...] = jnp.zeros((rows, HD), jnp.float32)
    acc_ref[...] = jnp.zeros((rows, HD), jnp.float32)
    token = base + lax.broadcasted_iota(jnp.int32, (tq, 1), 0)
    scale = HD ** (-0.5) * 1.4426950408889634

    def update(keys, values, mask):
        width = keys.shape[0]
        s = lax.dot_general(q, keys, (((1,), (1,)), ((), ())), preferred_element_type=jnp.float32)
        s = s.reshape(heads, tq, width) * scale
        s = jnp.where(mask[None], s, masked_score).reshape(rows, width)
        before = m_ref[...]
        peak = jnp.maximum(before, jnp.max(s, axis=1, keepdims=True))
        m_ref[...] = peak
        keep = jnp.exp2(before - peak)
        p = jnp.exp2(s - jnp.concatenate([peak] * (width // HD), axis=1))
        l_ref[...] = l_ref[...] * keep + jnp.sum(p, axis=1, keepdims=True)
        acc_ref[...] = acc_ref[...] * keep + jnp.dot(
            p.astype(jnp.bfloat16), values, preferred_element_type=jnp.float32
        )

    for r in range(REQ_REP):
        start, end, pref = scal[r], scal[REQ_REP + r], scal[2 * REQ_REP + r]
        inside = (token >= start) & (token < end)

        @pl.when((start < base + tq) & (end > base))
        def _(r=r, start=start, pref=pref, inside=inside):
            @pl.loop(0, (pref + tc - 1) // tc)
            def _(j):
                at = pl.ds(pl.multiple_of(r * PREF_MAX + j * tc, tc), tc)
                slot = j * tc + lax.broadcasted_iota(jnp.int32, (1, tc), 1)
                update(c_ref[at, :HD], c_ref[at, HD:], inside & (slot < pref))

            @pl.loop(start // tq, base // tq + 1)
            def _(j):
                at = pl.ds(pl.multiple_of(j * tq, tq), tq)
                other = j * tq + lax.broadcasted_iota(jnp.int32, (1, tq), 1)
                update(k_ref[at, :], v_ref[at, :], inside & (other >= start) & (other <= token))

    out = (acc_ref[...] / l_ref[...]).astype(jnp.bfloat16)
    for h in range(heads):
        o_ref[:, h * HD : (h + 1) * HD] = out[h * tq : (h + 1) * tq]


def attend(scal, q, k, v, cache, first, rows, tq=128, tc=256):
    heads = q.shape[1] // HD
    tokens, slots = q.shape[0], cache.shape[0]
    whole = lambda r, w: pl.BlockSpec((r, w), lambda i, *_: (0, 0))
    return pl.pallas_call(
        functools.partial(attend_kernel, first=first, heads=heads, tq=tq, tc=tc),
        out_shape=jax.ShapeDtypeStruct((rows, heads * HD), jnp.bfloat16),
        grid_spec=pltpu.PrefetchScalarGridSpec(
            num_scalar_prefetch=1,
            grid=(rows // tq,),
            in_specs=[
                pl.BlockSpec((tq, heads * HD), lambda i, *_: (first // tq + i, 0)),
                whole(tokens, HD),
                whole(tokens, HD),
                pl.BlockSpec((slots, 2 * HD), lambda i, s: (0, s[3 * REQ_REP])),
            ],
            out_specs=pl.BlockSpec((tq, heads * HD), lambda i, *_: (i, 0)),
            scratch_shapes=[pltpu.VMEM((heads * tq, HD), jnp.float32)] * 3,
        ),
        compiler_params=pltpu.CompilerParams(vmem_limit_bytes=VMEM_LIMIT),
        cost_estimate=pl.CostEstimate(
            flops=4 * rows * heads * HD * 1024,
            bytes_accessed=rows * heads * HD * 4 + slots * HD * 4 + tokens * HD * 4,
            transcendentals=rows * heads * 1024,
        ),
        name="attend",
    )(scal, q, k, v, cache)


def output_kernel(choice, a_ref, *rest, count, slots):
    pieces, (keep_ref, send_ref, held, sems) = rest[:count], rest[count:]

    for s in range(slots):
        for i in range(count):

            @pl.when(choice[s] == i)
            def _(s=s, i=i):
                pltpu.make_async_copy(pieces[i], held.at[s], sems.at[s]).start()

    half = slots // 2
    for s in range(slots):
        pltpu.make_async_copy(pieces[0], held.at[s], sems.at[s]).wait()
        part = jnp.dot(a_ref[...], held[s], preferred_element_type=jnp.float32)
        part = part.astype(jnp.bfloat16)
        if s < half:
            keep_ref[s] = part
        else:
            send_ref[s - half] = part


def output_parts(choice, attended, pieces, slots):
    rows, depth = attended.shape
    width = pieces[0].shape[1]
    count = len(pieces)
    half = jax.ShapeDtypeStruct((slots // 2, rows, width), jnp.bfloat16)
    vmem = pl.BlockSpec(memory_space=pltpu.VMEM)
    return pl.pallas_call(
        functools.partial(output_kernel, count=count, slots=slots),
        out_shape=[half, half],
        in_specs=[pl.BlockSpec(memory_space=pltpu.SMEM), vmem]
        + [pl.BlockSpec(memory_space=pl.ANY)] * count,
        out_specs=[vmem, vmem],
        scratch_shapes=[
            pltpu.VMEM((slots, depth, width), jnp.bfloat16),
            pltpu.SemaphoreType.DMA((slots,)),
        ],
        compiler_params=pltpu.CompilerParams(vmem_limit_bytes=VMEM_LIMIT),
        cost_estimate=pl.CostEstimate(
            flops=2 * rows * depth * width * slots,
            bytes_accessed=rows * depth * 2 + slots * width * (depth + rows) * 2,
            transcendentals=0,
        ),
        name="output_parts",
    )(choice, attended, *pieces)


def residual_kernel(where, h_ref, keep_ref, recv_ref, *rest):
    r_ref, ssq_ref = rest[-2:]
    proj = keep_ref[...].astype(jnp.float32) + recv_ref[...].astype(jnp.float32)
    resid = (h_ref[...].astype(jnp.float32) + proj).astype(jnp.bfloat16)
    r_ref[...] = resid
    wide = resid.astype(jnp.float32)
    square = wide * wide
    ssq = sum(square[:, i : i + HD] for i in range(0, square.shape[1], HD))
    if len(rest) > 2:
        ssq = ssq + rest[1][...]
    ssq_ref[...] = ssq


def residual_part(where, hidden, keep, recv, total_width, earlier=None, tile=256):
    rows = hidden.shape[0]
    width = keep.shape[1]
    block = pl.BlockSpec((tile, width), lambda i, *_: (i, 0))
    lanes = pl.BlockSpec((tile, HD), lambda i, *_: (i, 0))
    in_specs = [pl.BlockSpec((tile, width), lambda i, w: (i, w[1])), block, block]
    args = [hidden, keep, recv]
    aliases = {}
    if earlier is not None:
        in_specs += [pl.BlockSpec(memory_space=pl.ANY), lanes]
        args += list(earlier)
        aliases = {4: 0, 5: 1}
    return pl.pallas_call(
        residual_kernel,
        out_shape=[
            jax.ShapeDtypeStruct((rows, total_width), jnp.bfloat16),
            jax.ShapeDtypeStruct((rows, HD), jnp.float32),
        ],
        grid_spec=pltpu.PrefetchScalarGridSpec(
            num_scalar_prefetch=1,
            grid=(rows // tile,),
            in_specs=in_specs,
            out_specs=[pl.BlockSpec((tile, width), lambda i, w: (i, w[0])), lanes],
        ),
        input_output_aliases=aliases,
        compiler_params=pltpu.CompilerParams(vmem_limit_bytes=VMEM_LIMIT),
        cost_estimate=pl.CostEstimate(
            flops=6 * rows * width, bytes_accessed=rows * width * 8 + rows * HD * 8, transcendentals=0
        ),
        name="residual_part",
    )(where, *args)


def after(value, *others):
    return lax.optimization_barrier((value, *others))[0]


def body(hidden, norm_gain, w_query, w_keyval, w_output, cache, lengths, prefix, out_gain):
    n_rep, n_tp = lax.axis_size("rep"), lax.axis_size("tp")
    rep, tp = lax.axis_index("rep"), lax.axis_index("tp")
    rows, model = hidden.shape
    heads_here = w_query.shape[1] // HD
    order, source, piece, column, last = tables(n_rep, n_tp)
    ahead = [(order[i], order[(i + 1) % n_rep]) for i in range(n_rep)]
    back = [(b, a) for a, b in ahead]
    swap = lambda value, d: lax.ppermute(value, "tp", [(i, i ^ d) for i in range(n_tp)])
    step = lambda pair: (lax.ppermute(pair[0], "rep", ahead), lax.ppermute(pair[1], "rep", back))

    mid = w_output.shape[1] // 2
    out_pairs = [(w_output[:, :mid], w_output[:, mid:])]
    out_pairs.append(step(out_pairs[0]))

    kv_head_of = lambda t: t * heads_here // (H // KV)
    feats = w_keyval.shape[1] // KV
    col = jnp.arange(w_keyval.shape[1], dtype=jnp.int32)[:, None]
    feat = jnp.arange(feats, dtype=jnp.int32)[None, :]
    parts = []
    for d in range(n_tp):
        pick = (col == feat * KV + kv_head_of(tp ^ d)).astype(jnp.bfloat16)
        mine = jnp.dot(w_keyval, pick, preferred_element_type=jnp.float32).astype(jnp.bfloat16)
        parts.append(swap(mine, d) if d else mine)
    mixed = jnp.concatenate(parts, axis=1)
    slot = jnp.arange(mixed.shape[1], dtype=jnp.int32)
    home = ((slot // feats) ^ tp) * feats + slot % feats
    place = (home[:, None] == slot[None, :]).astype(jnp.bfloat16)
    keyval = jnp.dot(mixed, place, preferred_element_type=jnp.float32).astype(jnp.bfloat16)

    joined = jnp.concatenate([w_query, keyval], axis=1)
    depth = joined.shape[0] // 2
    in_pairs = [(joined[:depth], joined[depth:])]
    for _ in range(n_rep - 1):
        in_pairs.append(step(in_pairs[-1]))

    x = rms_scale(hidden.astype(jnp.float32), norm_gain.astype(jnp.float32)).astype(jnp.bfloat16)
    lens = lengths.reshape(-1)
    position, starts, ends = request_position(lens, prefix, rows)
    rope = rope_tables(position)
    scal = jnp.concatenate(
        [starts, ends, prefix, kv_head_of(tp).astype(jnp.int32)[None]]
    ).astype(jnp.int32)

    index = jnp.asarray(source)[rep]
    flat = [p for pair in in_pairs for p in pair]
    cut = n_rep
    acc = project(index[:cut], x, flat[:cut])
    q, k, v = project(index[cut:], x, flat[cut:], acc, rope)

    start = lax.optimization_barrier((*out_pairs[1], *in_pairs[-1]))
    out_pairs[1] = start[:2]
    for _ in range(n_rep - 2):
        out_pairs.append(step(out_pairs[-1]))

    n_parts = 4
    part_rows = rows // n_parts
    attended = jnp.concatenate(
        [attend(scal, q, k, v, cache, i * part_rows, part_rows) for i in range(n_parts)], axis=0
    )

    bits = n_tp.bit_length() - 1
    dests = tp ^ jnp.asarray([bit_reverse(s, bits) for s in range(n_tp)], jnp.int32)
    choice_all = jnp.asarray(piece)[rep][dests]
    column_all = jnp.asarray(column)[rep][tp]
    halves = piece.shape[2]
    flat_out = [p for pair in out_pairs for p in pair]
    earlier = None
    for s in range(halves):
        ready = flat_out[: 2 * (last[s] + 1)]
        keep, send = output_parts(choice_all[:, s], attended, ready, n_tp)
        slots, d = n_tp // 2, 1
        while slots > 1:
            total = (keep.astype(jnp.float32) + swap(send, d).astype(jnp.float32)).astype(
                jnp.bfloat16
            )
            slots, d = slots // 2, d * 2
            keep, send = total[:slots], total[slots:]
        recv = swap(send, d)
        where = jnp.stack([column_all[s], tp * halves + column_all[s]]).astype(jnp.int32)
        earlier = residual_part(
            where, hidden, keep[0], recv[0], model // n_tp, earlier
        )
    resid, lanes = earlier

    ssq = jnp.sum(lanes, axis=1)
    d = 1
    while d < n_tp:
        ssq = ssq + swap(ssq, d)
        d *= 2
    width = model // n_tp
    gain = lax.dynamic_slice_in_dim(out_gain, tp * width, width, 0).astype(jnp.float32)
    factor = lax.rsqrt(ssq / model + norm_eps)
    normed = (resid.astype(jnp.float32) * factor[:, None] * gain[None, :]).astype(jnp.bfloat16)
    return (resid, normed)


def solution(mesh):
    placed = (
        P("rep", None),
        P(),
        P("rep", "tp"),
        P("rep", "tp"),
        P("tp", "rep"),
        P("rep", None),
        P("rep", None),
        P("rep"),
        P(),
    )
    return jax.shard_map(
        body,
        mesh=mesh,
        in_specs=placed,
        out_specs=(P("rep", "tp"), P("rep", "tp")),
        check_vma=False,
    )
```

```python
import functools

import jax
import jax.numpy as jnp
import numpy as np
from jax import lax
from jax.experimental import pallas as pl
from jax.experimental.pallas import tpu as pltpu
from jax.sharding import PartitionSpec as P

H = 32
KV = 4
HD = 128
REQ_REP = 4
PREF_MAX = 512

norm_eps = 1e-05
rope_base = 5000000.0
masked_score = -1e30
lowest_peak = -1e25

VMEM_LIMIT = 63 * 1024 * 1024

SMALL = pl.CostEstimate(flops=1024, bytes_accessed=1024, transcendentals=0)


def ring_order(count):
    return list(range(0, count, 2)) + list(range(count - 1, 0, -2))


def bit_reverse(value, bits):
    return sum(((value >> b) & 1) << (bits - 1 - b) for b in range(bits))


def tables(n_rep, n_tp):
    order = ring_order(n_rep)
    place = [order.index(r) for r in range(n_rep)]
    halves = 2 * n_rep // n_tp
    source = np.zeros((n_rep, 2 * n_rep), np.int32)
    piece = np.zeros((n_rep, n_tp, halves), np.int32)
    column = np.zeros((n_rep, n_tp, halves), np.int32)
    last = [0] * halves
    for r in range(n_rep):
        seen = [0] * n_tp
        for k in range(n_rep):
            for h, src in ((0, order[(place[r] - k) % n_rep]), (1, order[(place[r] + k) % n_rep])):
                source[r, 2 * k + h] = src * 2 + h
                dest = src * n_tp // n_rep
                s = seen[dest]
                seen[dest] += 1
                piece[r, dest, s] = 2 * k + h
                column[r, dest, s] = src * 2 + h - dest * halves
                last[s] = max(last[s], k)
    return order, source, piece, column, last


def rope_tables(position):
    half = HD // 2
    freqs = rope_base ** (-(jnp.arange(half, dtype=jnp.float32) * 2.0 / HD))
    angles = position.astype(jnp.float32)[:, None] * freqs[None, :]
    cosine, sine = jnp.cos(angles), jnp.sin(angles)
    return jnp.concatenate([cosine, cosine], 1), jnp.concatenate([-sine, sine], 1)


def request_position(lens, prefs, count):
    token_ids = jnp.arange(count, dtype=jnp.int32)
    ends = jnp.cumsum(lens)
    starts = ends - lens
    segment = jnp.sum((token_ids[:, None] >= ends[None, :]).astype(jnp.int32), axis=1)
    onehot = segment[:, None] == jnp.arange(lens.shape[0], dtype=jnp.int32)[None, :]
    shift = jnp.sum(jnp.where(onehot, (prefs - starts)[None, :], 0), axis=1)
    return token_ids + shift, starts, ends


def skipping(kernel, first, count):
    return lambda *refs: kernel(*refs[:first], *refs[first + count :])


def norm_kernel(h_ref, gain_ref, *rest):
    out_ref = rest[-1]
    values = h_ref[...].astype(jnp.float32)
    meansq = jnp.mean(values * values, axis=-1, keepdims=True)
    gain = gain_ref[...].astype(jnp.float32)
    out_ref[...] = (values * lax.rsqrt(meansq + norm_eps) * gain).astype(jnp.bfloat16)


def input_norm(hidden, gain, also, tile=128):
    rows, model = hidden.shape
    block = pl.BlockSpec((tile, model), lambda i: (i, 0))
    return pl.pallas_call(
        norm_kernel,
        out_shape=jax.ShapeDtypeStruct((rows, model), jnp.bfloat16),
        grid=(rows // tile,),
        in_specs=[block, pl.BlockSpec((1, model), lambda i: (0, 0))]
        + [pl.BlockSpec(memory_space=pl.ANY)] * len(also),
        out_specs=block,
        compiler_params=pltpu.CompilerParams(vmem_limit_bytes=VMEM_LIMIT),
        cost_estimate=SMALL,
        name="input_norm",
    )(hidden, gain.reshape(1, model), *also)


def project_kernel(index, *refs, count, final, has_acc, heads):
    xs, pieces, rest = refs[:count], refs[count : 2 * count], refs[2 * count :]
    x = jnp.concatenate([ref[...] for ref in xs], axis=1)
    weights = jnp.concatenate([ref[...] for ref in pieces], axis=0)
    total = jnp.dot(x, weights, preferred_element_type=jnp.float32)
    if has_acc:
        total = total + rest[0][...]
        rest = rest[1:]
    if not final:
        rest[0][...] = total
        return
    cos_ref, sin_ref, q_ref, k_ref, v_ref = rest
    cosine, sine = cos_ref[...], sin_ref[...]

    def rotate(u):
        return (u * cosine + pltpu.roll(u, HD // 2, 1) * sine).astype(jnp.bfloat16)

    for h in range(heads):
        q_ref[:, h * HD : (h + 1) * HD] = rotate(total[:, h * HD : (h + 1) * HD])
    key = total[:, heads * HD : (heads + 1) * HD]
    k_ref[...] = rotate(key.astype(jnp.bfloat16).astype(jnp.float32))
    v_ref[...] = total[:, (heads + 1) * HD :].astype(jnp.bfloat16)


def project(index, x, pieces, acc=None, rope=None, also=(), tile=256):
    rows, model = x.shape
    depth, width = pieces[0].shape
    count = len(pieces)
    heads = width // HD - 2
    final = rope is not None
    row_block = lambda w: pl.BlockSpec((tile, w), lambda i, *_: (i, 0))
    in_specs = [
        pl.BlockSpec((tile, depth), lambda i, at, k=k: (i, at[k])) for k in range(count)
    ] + [pl.BlockSpec((depth, width), lambda i, *_: (0, 0), pipeline_mode=pl.Buffered(1))] * count
    args = [x] * count + list(pieces)
    if acc is not None:
        in_specs.append(row_block(width))
        args.append(acc)
    if final:
        in_specs += [row_block(HD)] * 2
        args += list(rope)
        out_shape = [
            jax.ShapeDtypeStruct((rows, heads * HD), jnp.bfloat16),
            jax.ShapeDtypeStruct((rows, HD), jnp.bfloat16),
            jax.ShapeDtypeStruct((rows, HD), jnp.bfloat16),
        ]
        out_specs = [row_block(heads * HD), row_block(HD), row_block(HD)]
    else:
        out_shape = jax.ShapeDtypeStruct((rows, width), jnp.float32)
        out_specs = row_block(width)
    kernel = functools.partial(
        project_kernel, count=count, final=final, has_acc=acc is not None, heads=heads
    )
    kernel = skipping(kernel, 1 + len(args), len(also))
    in_specs += [pl.BlockSpec(memory_space=pl.ANY)] * len(also)
    args += list(also)
    return pl.pallas_call(
        kernel,
        out_shape=out_shape,
        grid_spec=pltpu.PrefetchScalarGridSpec(
            num_scalar_prefetch=1, grid=(rows // tile,), in_specs=in_specs, out_specs=out_specs
        ),
        compiler_params=pltpu.CompilerParams(vmem_limit_bytes=VMEM_LIMIT),
        cost_estimate=SMALL,
        name="project",
    )(index, *args)


def attend_kernel(
    scal, q_ref, k_ref, v_ref, c_ref, *rest, first, heads, tq, tk
):
    o_ref, m_ref, acc_ref = rest[-3:]
    base = first + pl.program_id(0) * tq
    rows = heads * tq
    q = jnp.concatenate([q_ref[:, h * HD : (h + 1) * HD] for h in range(heads)], axis=0)
    m_ref[...] = jnp.full((rows, HD), lowest_peak, jnp.float32)
    acc_ref[...] = jnp.zeros((rows, 2 * HD), jnp.float32)
    token = base + lax.broadcasted_iota(jnp.int32, (tq, 1), 0)
    scale = HD ** (-0.5) * 1.4426950408889634

    def update(keys, values, mask):
        width = keys.shape[0]
        s = lax.dot_general(q, keys, (((1,), (1,)), ((), ())), preferred_element_type=jnp.float32)
        s = s.reshape(heads, tq, width) * scale
        s = jnp.where(mask[None], s, masked_score).reshape(rows, width)
        before = m_ref[...]
        peak = jnp.maximum(before, jnp.max(s, axis=1, keepdims=True))
        m_ref[...] = peak
        keep = jnp.exp2(before - peak)
        p = jnp.exp2(s - jnp.concatenate([peak] * (width // HD), axis=1)).astype(jnp.bfloat16)
        wide = jnp.concatenate([values, jnp.ones((width, HD), jnp.bfloat16)], axis=1)
        acc_ref[...] = acc_ref[...] * jnp.concatenate([keep, keep], axis=1) + jnp.dot(
            p, wide, preferred_element_type=jnp.float32
        )

    for r in range(REQ_REP):
        start, end, pref = scal[r], scal[REQ_REP + r], scal[2 * REQ_REP + r]
        inside = (token >= start) & (token < end)

        @pl.when((start < base + tq) & (end > base))
        def _(r=r, start=start, end=end, pref=pref, inside=inside):
            @pl.loop(0, (pref + tk - 1) // tk)
            def _(j):
                at = pl.ds(pl.multiple_of(r * PREF_MAX + j * tk, tk), tk)
                slot = j * tk + lax.broadcasted_iota(jnp.int32, (1, tk), 1)
                update(c_ref[at, :HD], c_ref[at, HD:], inside & (slot < pref))

            @pl.loop(start // tk, (jnp.minimum(end, base + tq) - 1) // tk + 1)
            def _(j):
                at = pl.ds(pl.multiple_of(j * tk, tk), tk)
                other = j * tk + lax.broadcasted_iota(jnp.int32, (1, tk), 1)
                update(k_ref[at, :], v_ref[at, :], inside & (other >= start) & (other <= token))

    out = (acc_ref[:, :HD] / acc_ref[:, HD:]).astype(jnp.bfloat16)
    for h in range(heads):
        o_ref[:, h * HD : (h + 1) * HD] = out[h * tq : (h + 1) * tq]


def attend(scal, q, k, v, cache, first, rows, earlier=None, also=(), tq=128, tk=256):
    heads = q.shape[1] // HD
    tokens, slots = q.shape[0], cache.shape[0]
    whole = lambda r, w: pl.BlockSpec((r, w), lambda i, *_: (0, 0))
    block = pl.BlockSpec((tq, heads * HD), lambda i, *_: (first // tq + i, 0))
    more = ([] if earlier is None else [earlier]) + list(also)
    return pl.pallas_call(
        functools.partial(attend_kernel, first=first, heads=heads, tq=tq, tk=tk),
        out_shape=jax.ShapeDtypeStruct((tokens, heads * HD), jnp.bfloat16),
        grid_spec=pltpu.PrefetchScalarGridSpec(
            num_scalar_prefetch=1,
            grid=(rows // tq,),
            in_specs=[
                block,
                whole(tokens, HD),
                whole(tokens, HD),
                pl.BlockSpec((slots, 2 * HD), lambda i, s: (0, s[3 * REQ_REP])),
            ]
            + [pl.BlockSpec(memory_space=pl.ANY)] * len(more),
            out_specs=block,
            scratch_shapes=[
                pltpu.VMEM((heads * tq, HD), jnp.float32),
                pltpu.VMEM((heads * tq, 2 * HD), jnp.float32),
            ],
        ),
        input_output_aliases={} if earlier is None else {5: 0},
        compiler_params=pltpu.CompilerParams(vmem_limit_bytes=VMEM_LIMIT),
        cost_estimate=SMALL,
        name="attend",
    )(scal, q, k, v, cache, *more)


def output_kernel(choice, a_ref, *rest, count, slots):
    pieces, (keep_ref, send_ref, held, sems) = rest[:count], rest[count:]
    width = keep_ref.shape[2]

    @pl.when(pl.program_id(0) == 0)
    def _():
        for s in range(slots):
            for i in range(count):

                @pl.when(choice[s] == i)
                def _(s=s, i=i):
                    pltpu.make_async_copy(
                        pieces[i], held.at[:, pl.ds(s * width, width)], sems.at[s]
                    ).start()

        for s in range(slots):
            pltpu.make_async_copy(
                pieces[0], held.at[:, pl.ds(s * width, width)], sems.at[s]
            ).wait()

    half = slots // 2
    part = jnp.dot(a_ref[...], held[...], preferred_element_type=jnp.float32)
    part = part.astype(jnp.bfloat16)
    for s in range(half):
        keep_ref[s] = part[:, s * width : (s + 1) * width]
        send_ref[s] = part[:, (half + s) * width : (half + s + 1) * width]


def output_parts(choice, attended, pieces, slots, also=(), tile=512):
    rows, depth = attended.shape
    width = pieces[0].shape[1]
    count = len(pieces)
    half = jax.ShapeDtypeStruct((slots // 2, rows, width), jnp.bfloat16)
    half_block = pl.BlockSpec((slots // 2, tile, width), lambda i, *_: (0, i, 0))
    kernel = functools.partial(output_kernel, count=count, slots=slots)
    return pl.pallas_call(
        skipping(kernel, 2 + count, len(also)),
        out_shape=[half, half],
        grid_spec=pltpu.PrefetchScalarGridSpec(
            num_scalar_prefetch=1,
            grid=(rows // tile,),
            in_specs=[pl.BlockSpec((tile, depth), lambda i, *_: (i, 0))]
            + [pl.BlockSpec(memory_space=pl.ANY)] * (count + len(also)),
            out_specs=[half_block, half_block],
            scratch_shapes=[
                pltpu.VMEM((depth, slots * width), jnp.bfloat16),
                pltpu.SemaphoreType.DMA((slots,)),
            ],
        ),
        compiler_params=pltpu.CompilerParams(vmem_limit_bytes=VMEM_LIMIT),
        cost_estimate=SMALL,
        name="output_parts",
    )(choice, attended, *pieces, *also)


def residual_kernel(where, h_ref, *rest, groups, last):
    keeps, recvs, rest = rest[:groups], rest[groups : 2 * groups], rest[2 * groups :]
    r_ref, ssq_ref = rest[-2:]
    width = keeps[0].shape[2]
    total = rest[1][...] if last else None
    place = 0
    for keep, recv in zip(keeps, recvs):
        for j in range(keep.shape[0]):
            at = slice(None) if last else pl.ds(pl.multiple_of(where[place] * width, width), width)
            place += 1
            proj = keep[j].astype(jnp.float32) + recv[j].astype(jnp.float32)
            resid = (h_ref[:, at].astype(jnp.float32) + proj).astype(jnp.bfloat16)
            r_ref[:, at] = resid
            wide = resid.astype(jnp.float32)
            square = wide * wide
            for i in range(0, width, HD):
                part = square[:, i : i + HD]
                total = part if total is None else total + part
    if last:
        total = lax.dot_general(
            jnp.ones((8, HD), jnp.float32),
            total,
            (((1,), (1,)), ((), ())),
            precision=lax.Precision.HIGHEST,
            preferred_element_type=jnp.float32,
        )
    ssq_ref[...] = total


def residual(where, hidden, keeps, recvs, total_width, earlier=None, tile=512):
    rows = hidden.shape[0]
    groups = len(keeps)
    width = keeps[0].shape[2]
    last = earlier is not None
    parts = [
        pl.BlockSpec((g.shape[0], tile, width), lambda i, *_: (0, i, 0)) for g in keeps + recvs
    ]
    lanes = pl.BlockSpec((tile, HD), lambda i, *_: (i, 0))
    if last:
        in_place = pl.BlockSpec((tile, width), lambda i, w: (i, w[1]))
        out_place = pl.BlockSpec((tile, width), lambda i, w: (i, w[0]))
        more, more_specs = list(earlier), [pl.BlockSpec(memory_space=pl.ANY), lanes]
        aliases = {2 + 2 * groups: 0}
        ssq_shape, ssq_block = (8, rows), pl.BlockSpec((8, tile), lambda i, *_: (0, i))
    else:
        count = where.shape[0] - 1
        in_place = pl.BlockSpec((tile, total_width), lambda i, w: (i, w[count]))
        out_place = pl.BlockSpec((tile, total_width), lambda i, *_: (i, 0))
        more, more_specs, aliases = [], [], {}
        ssq_shape, ssq_block = (rows, HD), lanes
    return pl.pallas_call(
        functools.partial(residual_kernel, groups=groups, last=last),
        out_shape=[
            jax.ShapeDtypeStruct((rows, total_width), jnp.bfloat16),
            jax.ShapeDtypeStruct(ssq_shape, jnp.float32),
        ],
        grid_spec=pltpu.PrefetchScalarGridSpec(
            num_scalar_prefetch=1,
            grid=(rows // tile,),
            in_specs=[in_place] + parts + more_specs,
            out_specs=[out_place, ssq_block],
        ),
        input_output_aliases=aliases,
        compiler_params=pltpu.CompilerParams(vmem_limit_bytes=VMEM_LIMIT),
        cost_estimate=SMALL,
        name="residual",
    )(where, hidden, *keeps, *recvs, *more)


def join_kernel(*refs):
    pass


def join(arrays, *others):
    anywhere = pl.BlockSpec(memory_space=pltpu.HBM)
    count = len(arrays)
    return tuple(
        pl.pallas_call(
            join_kernel,
            out_shape=[jax.ShapeDtypeStruct(p.shape, p.dtype) for p in arrays],
            in_specs=[anywhere] * count + [pl.BlockSpec(memory_space=pl.ANY)] * len(others),
            out_specs=[anywhere] * count,
            input_output_aliases={i: i for i in range(count)},
            compiler_params=pltpu.CompilerParams(vmem_limit_bytes=VMEM_LIMIT),
            cost_estimate=SMALL,
            name="join",
        )(*arrays, *others)
    )


def body(hidden, norm_gain, w_query, w_keyval, w_output, cache, lengths, prefix, out_gain):
    n_rep, n_tp = lax.axis_size("rep"), lax.axis_size("tp")
    rep, tp = lax.axis_index("rep"), lax.axis_index("tp")
    rows, model = hidden.shape
    heads_here = w_query.shape[1] // HD
    order, source, piece, column, last = tables(n_rep, n_tp)
    ahead = [(order[i], order[(i + 1) % n_rep]) for i in range(n_rep)]
    back = [(b, a) for a, b in ahead]
    swap = lambda value, d: lax.ppermute(value, "tp", [(i, i ^ d) for i in range(n_tp)])
    step = lambda pair: (lax.ppermute(pair[0], "rep", ahead), lax.ppermute(pair[1], "rep", back))

    mid = w_output.shape[1] // 2
    out_pairs = [(w_output[:, :mid], w_output[:, mid:])]
    out_pairs.append(step(out_pairs[0]))

    kv_head_of = lambda t: t * heads_here // (H // KV)
    feats = w_keyval.shape[1] // KV
    col = jnp.arange(w_keyval.shape[1], dtype=jnp.int32)[:, None]
    feat = jnp.arange(feats, dtype=jnp.int32)[None, :]
    parts = []
    for d in range(n_tp):
        pick = (col == feat * KV + kv_head_of(tp ^ d)).astype(jnp.bfloat16)
        mine = jnp.dot(w_keyval, pick, preferred_element_type=jnp.float32).astype(jnp.bfloat16)
        parts.append(swap(mine, d) if d else mine)
    mixed = jnp.concatenate(parts, axis=1)
    slot = jnp.arange(mixed.shape[1], dtype=jnp.int32)
    home = ((slot // feats) ^ tp) * feats + slot % feats
    place = (home[:, None] == slot[None, :]).astype(jnp.bfloat16)
    keyval = jnp.dot(mixed, place, preferred_element_type=jnp.float32).astype(jnp.bfloat16)

    joined = jnp.concatenate([w_query, keyval], axis=1)
    depth = joined.shape[0] // 2

    lens = lengths.reshape(-1)
    position, starts, ends = request_position(lens, prefix, rows)
    rope = rope_tables(position)
    scal = jnp.concatenate(
        [starts, ends, prefix, kv_head_of(tp).astype(jnp.int32)[None]]
    ).astype(jnp.int32)

    bits = n_tp.bit_length() - 1
    dests = tp ^ jnp.asarray([bit_reverse(s, bits) for s in range(n_tp)], jnp.int32)
    choice_all = jnp.asarray(piece)[rep][dests]
    column_all = jnp.asarray(column)[rep][tp]
    halves = piece.shape[2]
    choices = [choice_all[:, s] for s in range(halves)]
    where_early = jnp.concatenate([column_all[:-1], tp[None]]).astype(jnp.int32)
    where_last = jnp.stack([column_all[-1], tp * halves + column_all[-1]]).astype(jnp.int32)
    width = model // n_tp
    gain = lax.dynamic_slice_in_dim(out_gain, tp * width, width, 0).astype(jnp.float32)

    first_cut, second_cut = n_rep // 2, n_rep - 2
    index = jnp.asarray(source)[rep]
    cuts = [0, first_cut, second_cut, n_rep]
    indices = [index[2 * low : 2 * high] for low, high in zip(cuts[:-1], cuts[1:])]
    in_pairs = [join((joined[:depth], joined[depth:]), *out_pairs[1])]
    x = input_norm(hidden, norm_gain, in_pairs[0][:1])
    acc, done = None, 0

    def project_arrived(acc, done, rope=None, also=()):
        ready = [p for pair in in_pairs[done:] for p in pair]
        return project(indices[cuts.index(done)], x, ready, acc, rope, also)

    for k in range(1, n_rep):
        arrived = step(in_pairs[-1])
        if k == 2:
            arrived = join(arrived, x)
        if k == 3:
            arrived = join(
                arrived, scal, *rope, *choices, where_early, where_last, gain, *indices
            )
        if k in (first_cut, second_cut):
            acc, done = project_arrived(acc, done), k
            arrived = join(arrived, acc)
        in_pairs.append(arrived)

    out_pairs[1] = join(out_pairs[1], *in_pairs[-1])
    q, k, v = project_arrived(acc, done, rope, out_pairs[1][:1])

    keeps, recvs = [], []

    def stage(s, attended, also=()):
        pieces = [p for pair in out_pairs[: last[s] + 1] for p in pair]
        return output_parts(choices[s], attended, pieces, n_tp, also)

    def exchange(keep, send):
        size, d = keep.shape[0], 1
        while d < n_tp // 2:
            received = swap(send, d)
            size, d = size // 2, d * 2
            total = [
                (keep[i : i + 1].astype(jnp.float32) + received[i : i + 1].astype(jnp.float32)).astype(
                    jnp.bfloat16
                )
                for i in range(2 * size)
            ]
            if d < n_tp // 2:
                keep = jnp.concatenate(total[:size], 0)
                send = jnp.concatenate(total[size:], 0)
        keeps.extend(total[:size])
        return total[size:]

    def collect(raw):
        sends = exchange(*raw)
        recvs.extend(swap(part, n_tp // 2) for part in sends)
        return sends

    shares = [0, 3, 6, 8]
    tq = rows // shares[-1]
    attended, raw, pending = None, None, list(range(halves))
    for flight in range(2, n_rep):
        arrived = step(out_pairs[-1])
        own = list(out_pairs[-1][:1])
        waits = []
        if flight == 2:
            waits = [q]
        elif flight - 3 < len(shares) - 1:
            low, high = shares[flight - 3 : flight - 1]
            attended = attend(
                scal, q, k, v, cache, low * tq, (high - low) * tq, attended, own, tq=tq
            )
            waits = [attended]
        if flight > len(shares):
            gates, sent = list(own), []
            if raw is not None:
                gates, raw = gates + collect(raw), None
                sent = recvs[-1:]
            if last[pending[0]] < flight and len(pending) > 1:
                raw = stage(pending.pop(0), attended, gates)
                *arrived, passed = join((*arrived, raw[1]), *sent)
                raw, waits = (raw[0], passed), []
        out_pairs.append(join(arrived, *waits) if waits else tuple(arrived))

    while pending:
        gates = collect(raw) if raw is not None else []
        raw = stage(pending.pop(0), attended, gates)
    early = residual(where_early, hidden, keeps, recvs, width)
    older = recvs[-1:]
    keeps.clear()
    recvs.clear()
    keep, send = raw
    (send,) = join((send,), *older)
    collect((keep, send))
    resid, ssq = residual(where_last, hidden, keeps, recvs, width, early)

    d = 1
    while d < n_tp:
        ssq = ssq + swap(ssq, d)
        d *= 2
    factor = lax.rsqrt(ssq[0] / model + norm_eps)
    normed = (resid.astype(jnp.float32) * factor[:, None] * gain[None, :]).astype(jnp.bfloat16)
    return (resid, normed)


def solution(mesh):
    placed = (
        P("rep", None),
        P(),
        P("rep", "tp"),
        P("rep", "tp"),
        P("tp", "rep"),
        P("rep", None),
        P("rep", None),
        P("rep"),
        P(),
    )
    return jax.shard_map(
        body,
        mesh=mesh,
        in_specs=placed,
        out_specs=(P("rep", "tp"), P("rep", "tp")),
        check_vma=False,
    )
```

```python
import functools

import jax
import jax.numpy as jnp
import numpy as np
from jax import lax
from jax.experimental import pallas as pl
from jax.experimental.pallas import tpu as pltpu
from jax.sharding import PartitionSpec as P

H = 32
KV = 4
HD = 128
REQ_REP = 4
PREF_MAX = 512

norm_eps = 1e-05
rope_base = 5000000.0
masked_score = -1e30
lowest_peak = -1e25

VMEM_LIMIT = 63 * 1024 * 1024

SMALL = pl.CostEstimate(flops=1024, bytes_accessed=1024, transcendentals=0)


def ring_order(count):
    return list(range(0, count, 2)) + list(range(count - 1, 0, -2))


def bit_reverse(value, bits):
    return sum(((value >> b) & 1) << (bits - 1 - b) for b in range(bits))


def tables(n_rep, n_tp):
    order = ring_order(n_rep)
    place = [order.index(r) for r in range(n_rep)]
    halves = 2 * n_rep // n_tp
    source = np.zeros((n_rep, 2 * n_rep), np.int32)
    piece = np.zeros((n_rep, n_tp, halves), np.int32)
    column = np.zeros((n_rep, n_tp, halves), np.int32)
    last = [0] * halves
    for r in range(n_rep):
        seen = [0] * n_tp
        for k in range(n_rep):
            for h, src in ((0, order[(place[r] - k) % n_rep]), (1, order[(place[r] + k) % n_rep])):
                source[r, 2 * k + h] = src * 2 + h
                dest = src * n_tp // n_rep
                s = seen[dest]
                seen[dest] += 1
                piece[r, dest, s] = 2 * k + h
                column[r, dest, s] = src * 2 + h - dest * halves
                last[s] = max(last[s], k)
    return order, source, piece, column, last


def rope_tables(position):
    half = HD // 2
    freqs = rope_base ** (-(jnp.arange(half, dtype=jnp.float32) * 2.0 / HD))
    angles = position.astype(jnp.float32)[:, None] * freqs[None, :]
    cosine, sine = jnp.cos(angles), jnp.sin(angles)
    return jnp.concatenate([cosine, cosine], 1), jnp.concatenate([-sine, sine], 1)


def request_position(lens, prefs, count):
    token_ids = jnp.arange(count, dtype=jnp.int32)
    ends = jnp.cumsum(lens)
    starts = ends - lens
    segment = jnp.sum((token_ids[:, None] >= ends[None, :]).astype(jnp.int32), axis=1)
    onehot = segment[:, None] == jnp.arange(lens.shape[0], dtype=jnp.int32)[None, :]
    shift = jnp.sum(jnp.where(onehot, (prefs - starts)[None, :], 0), axis=1)
    return token_ids + shift, starts, ends


def skipping(kernel, first, count):
    return lambda *refs: kernel(*refs[:first], *refs[first + count :])


def norm_kernel(h_ref, gain_ref, *rest):
    out_ref = rest[-1]
    values = h_ref[...].astype(jnp.float32)
    meansq = jnp.mean(values * values, axis=-1, keepdims=True)
    gain = gain_ref[...].astype(jnp.float32)
    out_ref[...] = (values * lax.rsqrt(meansq + norm_eps) * gain).astype(jnp.bfloat16)


def input_norm(hidden, gain, also, tile=128):
    rows, model = hidden.shape
    block = pl.BlockSpec((tile, model), lambda i: (i, 0))
    return pl.pallas_call(
        norm_kernel,
        out_shape=jax.ShapeDtypeStruct((rows, model), jnp.bfloat16),
        grid=(rows // tile,),
        in_specs=[block, pl.BlockSpec((1, model), lambda i: (0, 0))]
        + [pl.BlockSpec(memory_space=pl.ANY)] * len(also),
        out_specs=block,
        compiler_params=pltpu.CompilerParams(vmem_limit_bytes=VMEM_LIMIT),
        cost_estimate=SMALL,
        name="input_norm",
    )(hidden, gain.reshape(1, model), *also)


def project_kernel(index, *refs, count, final, has_acc, heads):
    xs, pieces, rest = refs[:count], refs[count : 2 * count], refs[2 * count :]
    x = jnp.concatenate([ref[...] for ref in xs], axis=1)
    weights = jnp.concatenate([ref[...] for ref in pieces], axis=0)
    total = jnp.dot(x, weights, preferred_element_type=jnp.float32)
    if has_acc:
        total = total + rest[0][...]
        rest = rest[1:]
    if not final:
        rest[0][...] = total
        return
    cos_ref, sin_ref, q_ref, k_ref, v_ref = rest
    cosine, sine = cos_ref[...], sin_ref[...]

    def rotate(u):
        return (u * cosine + pltpu.roll(u, HD // 2, 1) * sine).astype(jnp.bfloat16)

    for h in range(heads):
        q_ref[:, h * HD : (h + 1) * HD] = rotate(total[:, h * HD : (h + 1) * HD])
    key = total[:, heads * HD : (heads + 1) * HD]
    k_ref[...] = rotate(key.astype(jnp.bfloat16).astype(jnp.float32))
    v_ref[...] = total[:, (heads + 1) * HD :].astype(jnp.bfloat16)


def project(index, x, pieces, acc=None, rope=None, also=(), tile=256):
    rows, model = x.shape
    depth, width = pieces[0].shape
    count = len(pieces)
    heads = width // HD - 2
    final = rope is not None
    row_block = lambda w: pl.BlockSpec((tile, w), lambda i, *_: (i, 0))
    in_specs = [
        pl.BlockSpec((tile, depth), lambda i, at, k=k: (i, at[k])) for k in range(count)
    ] + [pl.BlockSpec((depth, width), lambda i, *_: (0, 0), pipeline_mode=pl.Buffered(1))] * count
    args = [x] * count + list(pieces)
    if acc is not None:
        in_specs.append(row_block(width))
        args.append(acc)
    if final:
        in_specs += [row_block(HD)] * 2
        args += list(rope)
        out_shape = [
            jax.ShapeDtypeStruct((rows, heads * HD), jnp.bfloat16),
            jax.ShapeDtypeStruct((rows, HD), jnp.bfloat16),
            jax.ShapeDtypeStruct((rows, HD), jnp.bfloat16),
        ]
        out_specs = [row_block(heads * HD), row_block(HD), row_block(HD)]
    else:
        out_shape = jax.ShapeDtypeStruct((rows, width), jnp.float32)
        out_specs = row_block(width)
    kernel = functools.partial(
        project_kernel, count=count, final=final, has_acc=acc is not None, heads=heads
    )
    kernel = skipping(kernel, 1 + len(args), len(also))
    in_specs += [pl.BlockSpec(memory_space=pl.ANY)] * len(also)
    args += list(also)
    return pl.pallas_call(
        kernel,
        out_shape=out_shape,
        grid_spec=pltpu.PrefetchScalarGridSpec(
            num_scalar_prefetch=1, grid=(rows // tile,), in_specs=in_specs, out_specs=out_specs
        ),
        compiler_params=pltpu.CompilerParams(vmem_limit_bytes=VMEM_LIMIT),
        cost_estimate=SMALL,
        name="project",
    )(index, *args)


def attend_kernel(
    scal, q_ref, k_ref, v_ref, c_ref, *rest, first, heads, tq, tk
):
    o_ref, m_ref, acc_ref = rest[-3:]
    base = first + pl.program_id(0) * tq
    rows = heads * tq
    q = jnp.concatenate([q_ref[:, h * HD : (h + 1) * HD] for h in range(heads)], axis=0)
    m_ref[...] = jnp.full((rows, HD), lowest_peak, jnp.float32)
    acc_ref[...] = jnp.zeros((rows, 2 * HD), jnp.float32)
    token = base + lax.broadcasted_iota(jnp.int32, (tq, 1), 0)
    scale = HD ** (-0.5) * 1.4426950408889634

    def update(keys, values, mask):
        width = keys.shape[0]
        s = lax.dot_general(q, keys, (((1,), (1,)), ((), ())), preferred_element_type=jnp.float32)
        s = s.reshape(heads, tq, width) * scale
        s = jnp.where(mask[None], s, masked_score).reshape(rows, width)
        before = m_ref[...]
        peak = jnp.maximum(before, jnp.max(s, axis=1, keepdims=True))
        m_ref[...] = peak
        keep = jnp.exp2(before - peak)
        p = jnp.exp2(s - jnp.concatenate([peak] * (width // HD), axis=1)).astype(jnp.bfloat16)
        wide = jnp.concatenate([values, jnp.ones((width, HD), jnp.bfloat16)], axis=1)
        acc_ref[...] = acc_ref[...] * jnp.concatenate([keep, keep], axis=1) + jnp.dot(
            p, wide, preferred_element_type=jnp.float32
        )

    for r in range(REQ_REP):
        start, end, pref = scal[r], scal[REQ_REP + r], scal[2 * REQ_REP + r]
        inside = (token >= start) & (token < end)

        @pl.when((start < base + tq) & (end > base))
        def _(r=r, start=start, end=end, pref=pref, inside=inside):
            @pl.loop(0, (pref + tk - 1) // tk)
            def _(j):
                at = pl.ds(pl.multiple_of(r * PREF_MAX + j * tk, tk), tk)
                slot = j * tk + lax.broadcasted_iota(jnp.int32, (1, tk), 1)
                update(c_ref[at, :HD], c_ref[at, HD:], inside & (slot < pref))

            @pl.loop(start // tk, (jnp.minimum(end, base + tq) - 1) // tk + 1)
            def _(j):
                at = pl.ds(pl.multiple_of(j * tk, tk), tk)
                other = j * tk + lax.broadcasted_iota(jnp.int32, (1, tk), 1)
                update(k_ref[at, :], v_ref[at, :], inside & (other >= start) & (other <= token))

    out = (acc_ref[:, :HD] / acc_ref[:, HD:]).astype(jnp.bfloat16)
    for h in range(heads):
        o_ref[:, h * HD : (h + 1) * HD] = out[h * tq : (h + 1) * tq]


def attend(scal, q, k, v, cache, first, rows, earlier=None, also=(), tq=128, tk=256):
    heads = q.shape[1] // HD
    tokens, slots = q.shape[0], cache.shape[0]
    whole = lambda r, w: pl.BlockSpec((r, w), lambda i, *_: (0, 0))
    block = pl.BlockSpec((tq, heads * HD), lambda i, *_: (first // tq + i, 0))
    more = ([] if earlier is None else [earlier]) + list(also)
    return pl.pallas_call(
        functools.partial(attend_kernel, first=first, heads=heads, tq=tq, tk=tk),
        out_shape=jax.ShapeDtypeStruct((tokens, heads * HD), jnp.bfloat16),
        grid_spec=pltpu.PrefetchScalarGridSpec(
            num_scalar_prefetch=1,
            grid=(rows // tq,),
            in_specs=[
                block,
                whole(tokens, HD),
                whole(tokens, HD),
                pl.BlockSpec((slots, 2 * HD), lambda i, s: (0, s[3 * REQ_REP])),
            ]
            + [pl.BlockSpec(memory_space=pl.ANY)] * len(more),
            out_specs=block,
            scratch_shapes=[
                pltpu.VMEM((heads * tq, HD), jnp.float32),
                pltpu.VMEM((heads * tq, 2 * HD), jnp.float32),
            ],
        ),
        input_output_aliases={} if earlier is None else {5: 0},
        compiler_params=pltpu.CompilerParams(vmem_limit_bytes=VMEM_LIMIT),
        cost_estimate=SMALL,
        name="attend",
    )(scal, q, k, v, cache, *more)


def output_kernel(choice, a_ref, *rest, count, slots):
    pieces, outs, (held, sems) = rest[:count], rest[count : count + slots], rest[count + slots :]
    width = outs[0].shape[1]

    @pl.when(pl.program_id(0) == 0)
    def _():
        for s in range(slots):
            for i in range(count):

                @pl.when(choice[s] == i)
                def _(s=s, i=i):
                    pltpu.make_async_copy(
                        pieces[i], held.at[:, pl.ds(s * width, width)], sems.at[s]
                    ).start()

        for s in range(slots):
            pltpu.make_async_copy(
                pieces[0], held.at[:, pl.ds(s * width, width)], sems.at[s]
            ).wait()

    part = jnp.dot(a_ref[...], held[...], preferred_element_type=jnp.float32)
    part = part.astype(jnp.bfloat16)
    for s in range(slots):
        outs[s][...] = part[:, s * width : (s + 1) * width]


def output_parts(choice, attended, pieces, slots, also=(), tile=512):
    rows, depth = attended.shape
    width = pieces[0].shape[1]
    count = len(pieces)
    kernel = functools.partial(output_kernel, count=count, slots=slots)
    return pl.pallas_call(
        skipping(kernel, 2 + count, len(also)),
        out_shape=[jax.ShapeDtypeStruct((rows, width), jnp.bfloat16)] * slots,
        grid_spec=pltpu.PrefetchScalarGridSpec(
            num_scalar_prefetch=1,
            grid=(rows // tile,),
            in_specs=[pl.BlockSpec((tile, depth), lambda i, *_: (i, 0))]
            + [pl.BlockSpec(memory_space=pl.ANY)] * (count + len(also)),
            out_specs=[pl.BlockSpec((tile, width), lambda i, *_: (i, 0))] * slots,
            scratch_shapes=[
                pltpu.VMEM((depth, slots * width), jnp.bfloat16),
                pltpu.SemaphoreType.DMA((slots,)),
            ],
        ),
        compiler_params=pltpu.CompilerParams(vmem_limit_bytes=VMEM_LIMIT),
        cost_estimate=SMALL,
        name="output_parts",
    )(choice, attended, *pieces, *also)


def residual_kernel(where, h_ref, *rest, stages, last):
    terms, rest = rest[: 3 * stages], rest[3 * stages :]
    r_ref, ssq_ref = rest[-2:]
    width = terms[0].shape[1]
    total = rest[1][...] if last else None
    for s in range(stages):
        at = slice(None) if last else pl.ds(pl.multiple_of(where[s] * width, width), width)
        proj = sum(term[...].astype(jnp.float32) for term in terms[3 * s : 3 * s + 3])
        resid = (h_ref[:, at].astype(jnp.float32) + proj).astype(jnp.bfloat16)
        r_ref[:, at] = resid
        wide = resid.astype(jnp.float32)
        square = wide * wide
        for i in range(0, width, HD):
            part = square[:, i : i + HD]
            total = part if total is None else total + part
    if last:
        total = lax.dot_general(
            jnp.ones((8, HD), jnp.float32),
            total,
            (((1,), (1,)), ((), ())),
            precision=lax.Precision.HIGHEST,
            preferred_element_type=jnp.float32,
        )
    ssq_ref[...] = total


def residual(where, hidden, terms, total_width, earlier=None, tile=512):
    rows = hidden.shape[0]
    stages = len(terms)
    terms = [term for stage in terms for term in stage]
    width = terms[0].shape[1]
    last = earlier is not None
    parts = [pl.BlockSpec((tile, width), lambda i, *_: (i, 0))] * len(terms)
    lanes = pl.BlockSpec((tile, HD), lambda i, *_: (i, 0))
    if last:
        in_place = pl.BlockSpec((tile, width), lambda i, w: (i, w[1]))
        out_place = pl.BlockSpec((tile, width), lambda i, w: (i, w[0]))
        more, more_specs = list(earlier), [pl.BlockSpec(memory_space=pl.ANY), lanes]
        aliases = {2 + len(terms): 0}
        ssq_shape, ssq_block = (8, rows), pl.BlockSpec((8, tile), lambda i, *_: (0, i))
    else:
        count = where.shape[0] - 1
        in_place = pl.BlockSpec((tile, total_width), lambda i, w: (i, w[count]))
        out_place = pl.BlockSpec((tile, total_width), lambda i, *_: (i, 0))
        more, more_specs, aliases = [], [], {}
        ssq_shape, ssq_block = (rows, HD), lanes
    return pl.pallas_call(
        functools.partial(residual_kernel, stages=stages, last=last),
        out_shape=[
            jax.ShapeDtypeStruct((rows, total_width), jnp.bfloat16),
            jax.ShapeDtypeStruct(ssq_shape, jnp.float32),
        ],
        grid_spec=pltpu.PrefetchScalarGridSpec(
            num_scalar_prefetch=1,
            grid=(rows // tile,),
            in_specs=[in_place] + parts + more_specs,
            out_specs=[out_place, ssq_block],
        ),
        input_output_aliases=aliases,
        compiler_params=pltpu.CompilerParams(vmem_limit_bytes=VMEM_LIMIT),
        cost_estimate=SMALL,
        name="residual",
    )(where, hidden, *terms, *more)


def join_kernel(*refs):
    pass


def join(arrays, *others):
    anywhere = pl.BlockSpec(memory_space=pltpu.HBM)
    count = len(arrays)
    return tuple(
        pl.pallas_call(
            join_kernel,
            out_shape=[jax.ShapeDtypeStruct(p.shape, p.dtype) for p in arrays],
            in_specs=[anywhere] * count + [pl.BlockSpec(memory_space=pl.ANY)] * len(others),
            out_specs=[anywhere] * count,
            input_output_aliases={i: i for i in range(count)},
            compiler_params=pltpu.CompilerParams(vmem_limit_bytes=VMEM_LIMIT),
            cost_estimate=SMALL,
            name="join",
        )(*arrays, *others)
    )


def body(hidden, norm_gain, w_query, w_keyval, w_output, cache, lengths, prefix, out_gain):
    n_rep, n_tp = lax.axis_size("rep"), lax.axis_size("tp")
    rep, tp = lax.axis_index("rep"), lax.axis_index("tp")
    rows, model = hidden.shape
    heads_here = w_query.shape[1] // HD
    order, source, piece, column, last = tables(n_rep, n_tp)
    ahead = [(order[i], order[(i + 1) % n_rep]) for i in range(n_rep)]
    back = [(b, a) for a, b in ahead]
    swap = lambda value, d: lax.ppermute(value, "tp", [(i, i ^ d) for i in range(n_tp)])
    step = lambda pair: (lax.ppermute(pair[0], "rep", ahead), lax.ppermute(pair[1], "rep", back))

    mid = w_output.shape[1] // 2
    out_pairs = [(w_output[:, :mid], w_output[:, mid:])]
    out_pairs.append(step(out_pairs[0]))

    kv_head_of = lambda t: t * heads_here // (H // KV)
    feats = w_keyval.shape[1] // KV
    col = jnp.arange(w_keyval.shape[1], dtype=jnp.int32)[:, None]
    feat = jnp.arange(feats, dtype=jnp.int32)[None, :]
    parts = []
    for d in range(n_tp):
        pick = (col == feat * KV + kv_head_of(tp ^ d)).astype(jnp.bfloat16)
        mine = jnp.dot(w_keyval, pick, preferred_element_type=jnp.float32).astype(jnp.bfloat16)
        parts.append(swap(mine, d) if d else mine)
    mixed = jnp.concatenate(parts, axis=1)
    slot = jnp.arange(mixed.shape[1], dtype=jnp.int32)
    home = ((slot // feats) ^ tp) * feats + slot % feats
    place = (home[:, None] == slot[None, :]).astype(jnp.bfloat16)
    keyval = jnp.dot(mixed, place, preferred_element_type=jnp.float32).astype(jnp.bfloat16)

    joined = jnp.concatenate([w_query, keyval], axis=1)
    depth = joined.shape[0] // 2

    lens = lengths.reshape(-1)
    position, starts, ends = request_position(lens, prefix, rows)
    rope = rope_tables(position)
    scal = jnp.concatenate(
        [starts, ends, prefix, kv_head_of(tp).astype(jnp.int32)[None]]
    ).astype(jnp.int32)

    bits = n_tp.bit_length() - 1
    dests = tp ^ jnp.asarray([bit_reverse(s, bits) for s in range(n_tp)], jnp.int32)
    choice_all = jnp.asarray(piece)[rep][dests]
    column_all = jnp.asarray(column)[rep][tp]
    halves = piece.shape[2]
    choices = [choice_all[:, s] for s in range(halves)]
    where_early = jnp.concatenate([column_all[:-1], tp[None]]).astype(jnp.int32)
    where_last = jnp.stack([column_all[-1], tp * halves + column_all[-1]]).astype(jnp.int32)
    width = model // n_tp
    gain = lax.dynamic_slice_in_dim(out_gain, tp * width, width, 0).astype(jnp.float32)

    first_cut, second_cut = n_rep // 2, n_rep - 2
    index = jnp.asarray(source)[rep]
    cuts = [0, first_cut, second_cut, n_rep]
    indices = [index[2 * low : 2 * high] for low, high in zip(cuts[:-1], cuts[1:])]
    in_pairs = [join((joined[:depth], joined[depth:]), *out_pairs[1])]
    x = input_norm(hidden, norm_gain, in_pairs[0][:1])
    acc, done = None, 0

    def project_arrived(acc, done, rope=None, also=()):
        ready = [p for pair in in_pairs[done:] for p in pair]
        return project(indices[cuts.index(done)], x, ready, acc, rope, also)

    for k in range(1, n_rep):
        arrived = step(in_pairs[-1])
        if k == 2:
            arrived = join(arrived, x)
        if k == 3:
            arrived = join(
                arrived, scal, *rope, *choices, where_early, where_last, gain, *indices
            )
        if k in (first_cut, second_cut):
            acc, done = project_arrived(acc, done), k
            arrived = join(arrived, acc)
        in_pairs.append(arrived)

    out_pairs[1] = join(out_pairs[1], *in_pairs[-1])
    q, k, v = project_arrived(acc, done, rope, out_pairs[1][:1])

    def stage(s, attended, also=()):
        pieces = [p for pair in out_pairs[: last[s] + 1] for p in pair]
        return output_parts(choices[s], attended, pieces, n_tp, also)

    def exchange(parts):
        d = 1
        while True:
            half = len(parts) // 2
            received = [swap(part, d) for part in parts[half:]]
            if half == 2:
                return (parts[0], received[0]), (parts[1], received[1])
            parts, d = [add(a, b) for a, b in zip(parts[:half], received)], d * 2

    def add(a, b):
        return (a.astype(jnp.float32) + b.astype(jnp.float32)).astype(jnp.bfloat16)

    terms = []

    def collect(parts, pieces=1):
        stay, leave = exchange(parts)
        share = rows // pieces
        sends = [add(*(a[i : i + share] for a in leave)) for i in range(0, rows, share)]
        recvs = [swap(part, n_tp // 2) for part in sends]
        terms.append((*stay, recvs[0] if pieces == 1 else jnp.concatenate(recvs, axis=0)))
        return sends, recvs

    shares = [0, 3, 6, 8]
    tq = rows // shares[-1]
    attended, raw, pending = None, None, list(range(halves))
    for flight in range(2, n_rep):
        arrived = step(out_pairs[-1])
        own = list(out_pairs[-1][:1])
        waits = []
        if flight == 2:
            waits = [q]
        elif flight - 3 < len(shares) - 1:
            low, high = shares[flight - 3 : flight - 1]
            attended = attend(
                scal, q, k, v, cache, low * tq, (high - low) * tq, attended, own, tq=tq
            )
            waits = [attended]
        if flight > len(shares):
            gates = list(own)
            if raw is not None:
                sends, waits = collect(raw)
                gates, raw = gates + sends, None
            if last[pending[0]] < flight and len(pending) > 1:
                raw = stage(pending.pop(0), attended, gates)
                half = len(raw) // 2
                arrived = join((*arrived, *raw[half:]), *waits)
                raw, arrived, waits = [*raw[:half], *arrived[2:]], arrived[:2], []
        out_pairs.append(join(arrived, *waits) if waits else tuple(arrived))

    recvs = []
    while pending:
        gates = []
        if raw is not None:
            gates, recvs = collect(raw, 2)
        raw = stage(pending.pop(0), attended, gates)
    early = residual(where_early, hidden, terms, width)
    half = len(raw) // 2
    raw = [*raw[:half], *join(raw[half:], *recvs[:1])]
    collect(raw)
    resid, ssq = residual(where_last, hidden, terms[-1:], width, early)

    ssq = ssq[:1]
    ssq = ssq + sum(swap(ssq, d) for d in range(1, n_tp))
    factor = lax.rsqrt(ssq[0] / model + norm_eps)
    normed = (resid.astype(jnp.float32) * factor[:, None] * gain[None, :]).astype(jnp.bfloat16)
    return (resid, normed)


def solution(mesh):
    placed = (
        P("rep", None),
        P(),
        P("rep", "tp"),
        P("rep", "tp"),
        P("tp", "rep"),
        P("rep", None),
        P("rep", None),
        P("rep"),
        P(),
    )
    return jax.shard_map(
        body,
        mesh=mesh,
        in_specs=placed,
        out_specs=(P("rep", "tp"), P("rep", "tp")),
        check_vma=False,
    )
```

```python
import functools

import jax
import jax.numpy as jnp
import numpy as np
from jax import lax
from jax.experimental import pallas as pl
from jax.experimental.pallas import tpu as pltpu
from jax.sharding import PartitionSpec as P

H = 32
KV = 4
HD = 128
REQ_REP = 4
PREF_MAX = 512

norm_eps = 1e-05
rope_base = 5000000.0
masked_score = -1e30
lowest_peak = -1e25

VMEM_LIMIT = 63 * 1024 * 1024

SMALL = pl.CostEstimate(flops=1024, bytes_accessed=1024, transcendentals=0)


def ring_order(count):
    return list(range(0, count, 2)) + list(range(count - 1, 0, -2))


def bit_reverse(value, bits):
    return sum(((value >> b) & 1) << (bits - 1 - b) for b in range(bits))


def tables(n_rep, n_tp):
    order = ring_order(n_rep)
    place = [order.index(r) for r in range(n_rep)]
    halves = 2 * n_rep // n_tp
    source = np.zeros((n_rep, 2 * n_rep), np.int32)
    piece = np.zeros((n_rep, n_tp, halves), np.int32)
    column = np.zeros((n_rep, n_tp, halves), np.int32)
    last = [0] * halves
    for r in range(n_rep):
        seen = [0] * n_tp
        for k in range(n_rep):
            for h, src in ((0, order[(place[r] - k) % n_rep]), (1, order[(place[r] + k) % n_rep])):
                source[r, 2 * k + h] = src * 2 + h
                dest = src * n_tp // n_rep
                s = seen[dest]
                seen[dest] += 1
                piece[r, dest, s] = 2 * k + h
                column[r, dest, s] = src * 2 + h - dest * halves
                last[s] = max(last[s], k)
    return order, source, piece, column, last


def rope_tables(position):
    half = HD // 2
    freqs = rope_base ** (-(jnp.arange(half, dtype=jnp.float32) * 2.0 / HD))
    angles = position.astype(jnp.float32)[:, None] * freqs[None, :]
    cosine, sine = jnp.cos(angles), jnp.sin(angles)
    return jnp.concatenate([cosine, cosine], 1), jnp.concatenate([-sine, sine], 1)


def request_position(lens, prefs, count):
    token_ids = jnp.arange(count, dtype=jnp.int32)
    ends = jnp.cumsum(lens)
    starts = ends - lens
    segment = jnp.sum((token_ids[:, None] >= ends[None, :]).astype(jnp.int32), axis=1)
    onehot = segment[:, None] == jnp.arange(lens.shape[0], dtype=jnp.int32)[None, :]
    shift = jnp.sum(jnp.where(onehot, (prefs - starts)[None, :], 0), axis=1)
    return token_ids + shift, starts, ends


def skipping(kernel, first, count):
    return lambda *refs: kernel(*refs[:first], *refs[first + count :])


def norm_kernel(h_ref, gain_ref, *rest):
    out_ref = rest[-1]
    values = h_ref[...].astype(jnp.float32)
    meansq = jnp.mean(values * values, axis=-1, keepdims=True)
    gain = gain_ref[...].astype(jnp.float32)
    out_ref[...] = (values * lax.rsqrt(meansq + norm_eps) * gain).astype(jnp.bfloat16)


def input_norm(hidden, gain, also, tile=128):
    rows, model = hidden.shape
    block = pl.BlockSpec((tile, model), lambda i: (i, 0))
    return pl.pallas_call(
        norm_kernel,
        out_shape=jax.ShapeDtypeStruct((rows, model), jnp.bfloat16),
        grid=(rows // tile,),
        in_specs=[block, pl.BlockSpec((1, model), lambda i: (0, 0))]
        + [pl.BlockSpec(memory_space=pl.ANY)] * len(also),
        out_specs=block,
        compiler_params=pltpu.CompilerParams(vmem_limit_bytes=VMEM_LIMIT),
        cost_estimate=SMALL,
        name="input_norm",
    )(hidden, gain.reshape(1, model), *also)


def project_kernel(index, *refs, count, final, has_acc, heads):
    xs, pieces, rest = refs[:count], refs[count : 2 * count], refs[2 * count :]
    x = jnp.concatenate([ref[...] for ref in xs], axis=1)
    weights = jnp.concatenate([ref[...] for ref in pieces], axis=0)
    total = jnp.dot(x, weights, preferred_element_type=jnp.float32)
    if has_acc:
        total = total + rest[0][...]
        rest = rest[1:]
    if not final:
        rest[0][...] = total
        return
    cos_ref, sin_ref, q_ref, k_ref, v_ref = rest
    cosine, sine = cos_ref[...], sin_ref[...]

    def rotate(u):
        return (u * cosine + pltpu.roll(u, HD // 2, 1) * sine).astype(jnp.bfloat16)

    for h in range(heads):
        q_ref[:, h * HD : (h + 1) * HD] = rotate(total[:, h * HD : (h + 1) * HD])
    key = total[:, heads * HD : (heads + 1) * HD]
    k_ref[...] = rotate(key.astype(jnp.bfloat16).astype(jnp.float32))
    v_ref[...] = total[:, (heads + 1) * HD :].astype(jnp.bfloat16)


def project(index, x, pieces, acc=None, rope=None, also=(), tile=256):
    rows, model = x.shape
    depth, width = pieces[0].shape
    count = len(pieces)
    heads = width // HD - 2
    final = rope is not None
    row_block = lambda w: pl.BlockSpec((tile, w), lambda i, *_: (i, 0))
    in_specs = [
        pl.BlockSpec((tile, depth), lambda i, at, k=k: (i, at[k])) for k in range(count)
    ] + [pl.BlockSpec((depth, width), lambda i, *_: (0, 0), pipeline_mode=pl.Buffered(1))] * count
    args = [x] * count + list(pieces)
    if acc is not None:
        in_specs.append(row_block(width))
        args.append(acc)
    if final:
        in_specs += [row_block(HD)] * 2
        args += list(rope)
        out_shape = [
            jax.ShapeDtypeStruct((rows, heads * HD), jnp.bfloat16),
            jax.ShapeDtypeStruct((rows, HD), jnp.bfloat16),
            jax.ShapeDtypeStruct((rows, HD), jnp.bfloat16),
        ]
        out_specs = [row_block(heads * HD), row_block(HD), row_block(HD)]
    else:
        out_shape = jax.ShapeDtypeStruct((rows, width), jnp.float32)
        out_specs = row_block(width)
    kernel = functools.partial(
        project_kernel, count=count, final=final, has_acc=acc is not None, heads=heads
    )
    kernel = skipping(kernel, 1 + len(args), len(also))
    in_specs += [pl.BlockSpec(memory_space=pl.ANY)] * len(also)
    args += list(also)
    return pl.pallas_call(
        kernel,
        out_shape=out_shape,
        grid_spec=pltpu.PrefetchScalarGridSpec(
            num_scalar_prefetch=1, grid=(rows // tile,), in_specs=in_specs, out_specs=out_specs
        ),
        compiler_params=pltpu.CompilerParams(vmem_limit_bytes=VMEM_LIMIT),
        cost_estimate=SMALL,
        name="project",
    )(index, *args)


def attend_kernel(
    scal, q_ref, k_ref, v_ref, c_ref, *rest, first, heads, tq, tk
):
    o_ref, m_ref, acc_ref = rest[-3:]
    base = first + pl.program_id(0) * tq
    rows = heads * tq
    q = jnp.concatenate([q_ref[:, h * HD : (h + 1) * HD] for h in range(heads)], axis=0)
    m_ref[...] = jnp.full((rows, HD), lowest_peak, jnp.float32)
    acc_ref[...] = jnp.zeros((rows, 2 * HD), jnp.float32)
    token = base + lax.broadcasted_iota(jnp.int32, (tq, 1), 0)
    scale = HD ** (-0.5) * 1.4426950408889634

    def update(keys, values, mask):
        width = keys.shape[0]
        s = lax.dot_general(q, keys, (((1,), (1,)), ((), ())), preferred_element_type=jnp.float32)
        s = s.reshape(heads, tq, width) * scale
        s = jnp.where(mask[None], s, masked_score).reshape(rows, width)
        before = m_ref[...]
        peak = jnp.maximum(before, jnp.max(s, axis=1, keepdims=True))
        m_ref[...] = peak
        keep = jnp.exp2(before - peak)
        p = jnp.exp2(s - jnp.concatenate([peak] * (width // HD), axis=1)).astype(jnp.bfloat16)
        wide = jnp.concatenate([values, jnp.ones((width, HD), jnp.bfloat16)], axis=1)
        acc_ref[...] = acc_ref[...] * jnp.concatenate([keep, keep], axis=1) + jnp.dot(
            p, wide, preferred_element_type=jnp.float32
        )

    for r in range(REQ_REP):
        start, end, pref = scal[r], scal[REQ_REP + r], scal[2 * REQ_REP + r]
        inside = (token >= start) & (token < end)

        @pl.when((start < base + tq) & (end > base))
        def _(r=r, start=start, end=end, pref=pref, inside=inside):
            @pl.loop(0, (pref + tk - 1) // tk)
            def _(j):
                at = pl.ds(pl.multiple_of(r * PREF_MAX + j * tk, tk), tk)
                slot = j * tk + lax.broadcasted_iota(jnp.int32, (1, tk), 1)
                update(c_ref[at, :HD], c_ref[at, HD:], inside & (slot < pref))

            @pl.loop(start // tk, (jnp.minimum(end, base + tq) - 1) // tk + 1)
            def _(j):
                at = pl.ds(pl.multiple_of(j * tk, tk), tk)
                other = j * tk + lax.broadcasted_iota(jnp.int32, (1, tk), 1)
                update(k_ref[at, :], v_ref[at, :], inside & (other >= start) & (other <= token))

    out = (acc_ref[:, :HD] / acc_ref[:, HD:]).astype(jnp.bfloat16)
    for h in range(heads):
        o_ref[:, h * HD : (h + 1) * HD] = out[h * tq : (h + 1) * tq]


def attend(scal, q, k, v, cache, first, rows, earlier=None, also=(), tq=128, tk=256):
    heads = q.shape[1] // HD
    tokens, slots = q.shape[0], cache.shape[0]
    whole = lambda r, w: pl.BlockSpec((r, w), lambda i, *_: (0, 0))
    block = pl.BlockSpec((tq, heads * HD), lambda i, *_: (first // tq + i, 0))
    more = ([] if earlier is None else [earlier]) + list(also)
    return pl.pallas_call(
        functools.partial(attend_kernel, first=first, heads=heads, tq=tq, tk=tk),
        out_shape=jax.ShapeDtypeStruct((tokens, heads * HD), jnp.bfloat16),
        grid_spec=pltpu.PrefetchScalarGridSpec(
            num_scalar_prefetch=1,
            grid=(rows // tq,),
            in_specs=[
                block,
                whole(tokens, HD),
                whole(tokens, HD),
                pl.BlockSpec((slots, 2 * HD), lambda i, s: (0, s[3 * REQ_REP])),
            ]
            + [pl.BlockSpec(memory_space=pl.ANY)] * len(more),
            out_specs=block,
            scratch_shapes=[
                pltpu.VMEM((heads * tq, HD), jnp.float32),
                pltpu.VMEM((heads * tq, 2 * HD), jnp.float32),
            ],
        ),
        input_output_aliases={} if earlier is None else {5: 0},
        compiler_params=pltpu.CompilerParams(vmem_limit_bytes=VMEM_LIMIT),
        cost_estimate=SMALL,
        name="attend",
    )(scal, q, k, v, cache, *more)


def output_kernel(choice, a_ref, *rest, count, slots):
    pieces, outs, (held, sems) = rest[:count], rest[count : count + slots], rest[count + slots :]
    width = outs[0].shape[1]

    @pl.when(pl.program_id(0) == 0)
    def _():
        for s in range(slots):
            for i in range(count):

                @pl.when(choice[s] == i)
                def _(s=s, i=i):
                    pltpu.make_async_copy(
                        pieces[i], held.at[:, pl.ds(s * width, width)], sems.at[s]
                    ).start()

        for s in range(slots):
            pltpu.make_async_copy(
                pieces[0], held.at[:, pl.ds(s * width, width)], sems.at[s]
            ).wait()

    part = jnp.dot(a_ref[...], held[...], preferred_element_type=jnp.float32)
    part = part.astype(jnp.bfloat16)
    for s in range(slots):
        outs[s][...] = part[:, s * width : (s + 1) * width]


def output_parts(choice, attended, pieces, slots, also=(), tile=512):
    rows, depth = attended.shape
    width = pieces[0].shape[1]
    count = len(pieces)
    kernel = functools.partial(output_kernel, count=count, slots=slots)
    return pl.pallas_call(
        skipping(kernel, 2 + count, len(also)),
        out_shape=[jax.ShapeDtypeStruct((rows, width), jnp.bfloat16)] * slots,
        grid_spec=pltpu.PrefetchScalarGridSpec(
            num_scalar_prefetch=1,
            grid=(rows // tile,),
            in_specs=[pl.BlockSpec((tile, depth), lambda i, *_: (i, 0))]
            + [pl.BlockSpec(memory_space=pl.ANY)] * (count + len(also)),
            out_specs=[pl.BlockSpec((tile, width), lambda i, *_: (i, 0))] * slots,
            scratch_shapes=[
                pltpu.VMEM((depth, slots * width), jnp.bfloat16),
                pltpu.SemaphoreType.DMA((slots,)),
            ],
        ),
        compiler_params=pltpu.CompilerParams(vmem_limit_bytes=VMEM_LIMIT),
        cost_estimate=SMALL,
        name="output_parts",
    )(choice, attended, *pieces, *also)


def residual_kernel(where, h_ref, *rest, stages, last):
    terms, rest = rest[: 3 * stages], rest[3 * stages :]
    r_ref, ssq_ref = rest[-2:]
    width = terms[0].shape[1]
    total = rest[1][...] if last else None
    for s in range(stages):
        at = slice(None) if last else pl.ds(pl.multiple_of(where[s] * width, width), width)
        proj = sum(term[...].astype(jnp.float32) for term in terms[3 * s : 3 * s + 3])
        resid = (h_ref[:, at].astype(jnp.float32) + proj).astype(jnp.bfloat16)
        r_ref[:, at] = resid
        wide = resid.astype(jnp.float32)
        square = wide * wide
        for i in range(0, width, HD):
            part = square[:, i : i + HD]
            total = part if total is None else total + part
    if last:
        total = lax.dot_general(
            jnp.ones((8, HD), jnp.float32),
            total,
            (((1,), (1,)), ((), ())),
            precision=lax.Precision.HIGHEST,
            preferred_element_type=jnp.float32,
        )
    ssq_ref[...] = total


def residual(where, hidden, terms, total_width, earlier=None, tile=512):
    rows = hidden.shape[0]
    stages = len(terms)
    terms = [term for stage in terms for term in stage]
    width = terms[0].shape[1]
    last = earlier is not None
    parts = [pl.BlockSpec((tile, width), lambda i, *_: (i, 0))] * len(terms)
    lanes = pl.BlockSpec((tile, HD), lambda i, *_: (i, 0))
    if last:
        in_place = pl.BlockSpec((tile, width), lambda i, w: (i, w[1]))
        out_place = pl.BlockSpec((tile, width), lambda i, w: (i, w[0]))
        more, more_specs = list(earlier), [pl.BlockSpec(memory_space=pl.ANY), lanes]
        aliases = {2 + len(terms): 0}
        ssq_shape, ssq_block = (8, rows), pl.BlockSpec((8, tile), lambda i, *_: (0, i))
    else:
        count = where.shape[0] - 1
        in_place = pl.BlockSpec((tile, total_width), lambda i, w: (i, w[count]))
        out_place = pl.BlockSpec((tile, total_width), lambda i, *_: (i, 0))
        more, more_specs, aliases = [], [], {}
        ssq_shape, ssq_block = (rows, HD), lanes
    return pl.pallas_call(
        functools.partial(residual_kernel, stages=stages, last=last),
        out_shape=[
            jax.ShapeDtypeStruct((rows, total_width), jnp.bfloat16),
            jax.ShapeDtypeStruct(ssq_shape, jnp.float32),
        ],
        grid_spec=pltpu.PrefetchScalarGridSpec(
            num_scalar_prefetch=1,
            grid=(rows // tile,),
            in_specs=[in_place] + parts + more_specs,
            out_specs=[out_place, ssq_block],
        ),
        input_output_aliases=aliases,
        compiler_params=pltpu.CompilerParams(vmem_limit_bytes=VMEM_LIMIT),
        cost_estimate=SMALL,
        name="residual",
    )(where, hidden, *terms, *more)


def output_norm_kernel(*refs, count, model):
    squares, (r_ref, gain_ref, out_ref) = refs[:count], refs[count:]
    total = lax.dot_general(
        jnp.concatenate([ref[...] for ref in squares], axis=0),
        jnp.ones((8 * count, HD), jnp.float32),
        (((0,), (0,)), ((), ())),
        precision=lax.Precision.HIGHEST,
        preferred_element_type=jnp.float32,
    )
    factor = lax.rsqrt(total * (1.0 / (8 * model)) + norm_eps)
    for i in range(0, r_ref.shape[1], HD):
        at = slice(i, i + HD)
        out_ref[:, at] = (r_ref[:, at].astype(jnp.float32) * factor * gain_ref[:, at]).astype(
            jnp.bfloat16
        )


def output_norm(squares, resid, gain, model, tile=512):
    rows, width = resid.shape
    block = pl.BlockSpec((tile, width), lambda i: (i, 0))
    return pl.pallas_call(
        functools.partial(output_norm_kernel, count=len(squares), model=model),
        out_shape=jax.ShapeDtypeStruct((rows, width), jnp.bfloat16),
        grid=(rows // tile,),
        in_specs=[pl.BlockSpec((8, tile), lambda i: (0, i))] * len(squares)
        + [block, pl.BlockSpec((1, width), lambda i: (0, 0))],
        out_specs=block,
        compiler_params=pltpu.CompilerParams(vmem_limit_bytes=VMEM_LIMIT),
        cost_estimate=SMALL,
        name="output_norm",
    )(*squares, resid, gain)


def join_kernel(*refs):
    pass


def join(arrays, *others):
    anywhere = pl.BlockSpec(memory_space=pltpu.HBM)
    count = len(arrays)
    return tuple(
        pl.pallas_call(
            join_kernel,
            out_shape=[jax.ShapeDtypeStruct(p.shape, p.dtype) for p in arrays],
            in_specs=[anywhere] * count + [pl.BlockSpec(memory_space=pl.ANY)] * len(others),
            out_specs=[anywhere] * count,
            input_output_aliases={i: i for i in range(count)},
            compiler_params=pltpu.CompilerParams(vmem_limit_bytes=VMEM_LIMIT),
            cost_estimate=SMALL,
            name="join",
        )(*arrays, *others)
    )


def body(hidden, norm_gain, w_query, w_keyval, w_output, cache, lengths, prefix, out_gain):
    n_rep, n_tp = lax.axis_size("rep"), lax.axis_size("tp")
    rep, tp = lax.axis_index("rep"), lax.axis_index("tp")
    rows, model = hidden.shape
    heads_here = w_query.shape[1] // HD
    order, source, piece, column, last = tables(n_rep, n_tp)
    ahead = [(order[i], order[(i + 1) % n_rep]) for i in range(n_rep)]
    back = [(b, a) for a, b in ahead]
    swap = lambda value, d: lax.ppermute(value, "tp", [(i, i ^ d) for i in range(n_tp)])
    step = lambda pair: (lax.ppermute(pair[0], "rep", ahead), lax.ppermute(pair[1], "rep", back))

    mid = w_output.shape[1] // 2
    out_pairs = [(w_output[:, :mid], w_output[:, mid:])]
    out_pairs.append(step(out_pairs[0]))

    kv_head_of = lambda t: t * heads_here // (H // KV)
    feats = w_keyval.shape[1] // KV
    col = jnp.arange(w_keyval.shape[1], dtype=jnp.int32)[:, None]
    feat = jnp.arange(feats, dtype=jnp.int32)[None, :]
    parts = []
    for d in range(n_tp):
        pick = (col == feat * KV + kv_head_of(tp ^ d)).astype(jnp.bfloat16)
        mine = jnp.dot(w_keyval, pick, preferred_element_type=jnp.float32).astype(jnp.bfloat16)
        parts.append(swap(mine, d) if d else mine)
    mixed = jnp.concatenate(parts, axis=1)
    slot = jnp.arange(mixed.shape[1], dtype=jnp.int32)
    home = ((slot // feats) ^ tp) * feats + slot % feats
    place = (home[:, None] == slot[None, :]).astype(jnp.bfloat16)
    keyval = jnp.dot(mixed, place, preferred_element_type=jnp.float32).astype(jnp.bfloat16)

    joined = jnp.concatenate([w_query, keyval], axis=1)
    depth = joined.shape[0] // 2

    lens = lengths.reshape(-1)
    position, starts, ends = request_position(lens, prefix, rows)
    rope = rope_tables(position)
    scal = jnp.concatenate(
        [starts, ends, prefix, kv_head_of(tp).astype(jnp.int32)[None]]
    ).astype(jnp.int32)

    bits = n_tp.bit_length() - 1
    dests = tp ^ jnp.asarray([bit_reverse(s, bits) for s in range(n_tp)], jnp.int32)
    choice_all = jnp.asarray(piece)[rep][dests]
    column_all = jnp.asarray(column)[rep][tp]
    halves = piece.shape[2]
    choices = [choice_all[:, s] for s in range(halves)]
    where_early = jnp.concatenate([column_all[:-1], tp[None]]).astype(jnp.int32)
    where_last = jnp.stack([column_all[-1], tp * halves + column_all[-1]]).astype(jnp.int32)
    width = model // n_tp
    gain = lax.dynamic_slice_in_dim(out_gain, tp * width, width, 0).astype(jnp.float32).reshape(1, width)

    first_cut, second_cut = n_rep // 2, n_rep - 2
    index = jnp.asarray(source)[rep]
    cuts = [0, first_cut, second_cut, n_rep]
    indices = [index[2 * low : 2 * high] for low, high in zip(cuts[:-1], cuts[1:])]
    in_pairs = [join((joined[:depth], joined[depth:]), *out_pairs[1])]
    x = input_norm(hidden, norm_gain, in_pairs[0][:1])
    acc, done = None, 0

    def project_arrived(acc, done, rope=None, also=()):
        ready = [p for pair in in_pairs[done:] for p in pair]
        return project(indices[cuts.index(done)], x, ready, acc, rope, also)

    for k in range(1, n_rep):
        arrived = step(in_pairs[-1])
        if k == 2:
            arrived = join(arrived, x)
        if k == 3:
            arrived = join(
                arrived, scal, *rope, *choices, where_early, where_last, gain, *indices
            )
        if k in (first_cut, second_cut):
            acc, done = project_arrived(acc, done), k
            arrived = join(arrived, acc)
        in_pairs.append(arrived)

    out_pairs[1] = join(out_pairs[1], *in_pairs[-1])
    q, k, v = project_arrived(acc, done, rope, out_pairs[1][:1])

    def stage(members, attended, also=()):
        pieces = [p for pair in out_pairs[: last[members[-1]] + 1] for p in pair]
        choice = jnp.stack([choices[s] for s in members], axis=1).reshape(-1)
        return output_parts(choice, attended, pieces, choice.shape[0], also)

    def exchange(parts, count):
        d = 1
        while True:
            half = len(parts) // 2
            received = [swap(part, d) for part in parts[half:]]
            pairs = list(zip(parts[:half], received))
            if half == 2 * count:
                return pairs[:count], pairs[count:]
            parts, d = [add(*pair) for pair in pairs], d * 2

    def add(a, b):
        return (a.astype(jnp.float32) + b.astype(jnp.float32)).astype(jnp.bfloat16)

    terms = []

    def collect(parts, pieces=1):
        share = rows // pieces
        all_sends, all_recvs = [], []
        for stay, leave in zip(*exchange(parts, len(parts) // n_tp)):
            sends = [add(*(a[i : i + share] for a in leave)) for i in range(0, rows, share)]
            recvs = [swap(part, n_tp // 2) for part in sends]
            terms.append((*stay, recvs[0] if pieces == 1 else jnp.concatenate(recvs, axis=0)))
            all_sends += sends
            all_recvs += recvs
        return all_sends, all_recvs

    shares = [0, 3, 6, 8]
    tq = rows // shares[-1]
    attended, raw, sent, pending = None, None, [], [[s] for s in range(halves)]
    if halves > 3:
        pending[:2] = [[0, 1]]
    for flight in range(2, n_rep):
        arrived = step(out_pairs[-1])
        own = list(out_pairs[-1][:1])
        waits = []
        if flight == 2:
            waits = [q]
        elif flight - 3 < len(shares) - 1:
            low, high = shares[flight - 3 : flight - 1]
            attended = attend(
                scal, q, k, v, cache, low * tq, (high - low) * tq, attended, own, tq=tq
            )
            waits = [attended]
        if flight > len(shares):
            gates = [*own, *sent[:1]]
            waits += sent[1:]
            sent = []
            if raw is not None:
                sends, sent = collect(raw)
                waits, raw = waits + sends, None
            elif last[pending[0][-1]] < flight and len(pending) > 1:
                raw = stage(pending.pop(0), attended, gates)
                half = len(raw) // 2
                arrived = join((*arrived, *raw[half:]), *waits)
                raw, arrived, waits = [*raw[:half], *arrived[2:]], arrived[:2], []
        out_pairs.append(join(arrived, *waits) if waits else tuple(arrived))

    recvs = []
    while pending:
        gates = []
        if raw is not None:
            gates, recvs = collect(raw, 2)
        raw = stage(pending.pop(0), attended, gates)
    early = residual(where_early, hidden, terms, width)
    half = len(raw) // 2
    raw = [*raw[:half], *join(raw[half:], *recvs[:1])]
    collect(raw)
    resid, ssq = residual(where_last, hidden, terms[-1:], width, early)

    squares = [ssq] + [swap(ssq, d) for d in range(1, n_tp)]
    normed = output_norm(squares, resid, gain, model)
    return (resid, normed)


def solution(mesh):
    placed = (
        P("rep", None),
        P(),
        P("rep", "tp"),
        P("rep", "tp"),
        P("tp", "rep"),
        P("rep", None),
        P("rep", None),
        P("rep"),
        P(),
    )
    return jax.shard_map(
        body,
        mesh=mesh,
        in_specs=placed,
        out_specs=(P("rep", "tp"), P("rep", "tp")),
        check_vma=False,
    )
```

```python
import functools

import jax
import jax.numpy as jnp
import numpy as np
from jax import lax
from jax.experimental import pallas as pl
from jax.experimental.pallas import tpu as pltpu
from jax.sharding import PartitionSpec as P

H = 32
KV = 4
HD = 128
REQ_REP = 4
PREF_MAX = 512

norm_eps = 1e-05
rope_base = 5000000.0
masked_score = -1e30
lowest_peak = -1e25

VMEM_LIMIT = 63 * 1024 * 1024

SMALL = pl.CostEstimate(flops=1024, bytes_accessed=1024, transcendentals=0)


def ring_order(count):
    return list(range(0, count, 2)) + list(range(count - 1, 0, -2))


def bit_reverse(value, bits):
    return sum(((value >> b) & 1) << (bits - 1 - b) for b in range(bits))


def tables(n_rep, n_tp):
    order = ring_order(n_rep)
    place = [order.index(r) for r in range(n_rep)]
    halves = 2 * n_rep // n_tp
    source = np.zeros((n_rep, 2 * n_rep), np.int32)
    piece = np.zeros((n_rep, n_tp, halves), np.int32)
    column = np.zeros((n_rep, n_tp, halves), np.int32)
    last = [0] * halves
    for r in range(n_rep):
        seen = [0] * n_tp
        for k in range(n_rep):
            for h, src in ((0, order[(place[r] - k) % n_rep]), (1, order[(place[r] + k) % n_rep])):
                source[r, 2 * k + h] = src * 2 + h
                dest = src * n_tp // n_rep
                s = seen[dest]
                seen[dest] += 1
                piece[r, dest, s] = 2 * k + h
                column[r, dest, s] = src * 2 + h - dest * halves
                last[s] = max(last[s], k)
    return order, source, piece, column, last


def rope_tables(position):
    half = HD // 2
    freqs = rope_base ** (-(jnp.arange(half, dtype=jnp.float32) * 2.0 / HD))
    angles = position.astype(jnp.float32)[:, None] * freqs[None, :]
    cosine, sine = jnp.cos(angles), jnp.sin(angles)
    return jnp.concatenate([cosine, cosine], 1), jnp.concatenate([-sine, sine], 1)


def request_position(lens, prefs, count):
    token_ids = jnp.arange(count, dtype=jnp.int32)
    ends = jnp.cumsum(lens)
    starts = ends - lens
    segment = jnp.sum((token_ids[:, None] >= ends[None, :]).astype(jnp.int32), axis=1)
    onehot = segment[:, None] == jnp.arange(lens.shape[0], dtype=jnp.int32)[None, :]
    shift = jnp.sum(jnp.where(onehot, (prefs - starts)[None, :], 0), axis=1)
    return token_ids + shift, starts, ends


def skipping(kernel, first, count):
    return lambda *refs: kernel(*refs[:first], *refs[first + count :])


def norm_kernel(h_ref, gain_ref, *rest):
    out_ref = rest[-1]
    values = h_ref[...].astype(jnp.float32)
    meansq = jnp.mean(values * values, axis=-1, keepdims=True)
    gain = gain_ref[...].astype(jnp.float32)
    out_ref[...] = (values * lax.rsqrt(meansq + norm_eps) * gain).astype(jnp.bfloat16)


def input_norm(hidden, gain, also, tile=128):
    rows, model = hidden.shape
    block = pl.BlockSpec((tile, model), lambda i: (i, 0))
    return pl.pallas_call(
        norm_kernel,
        out_shape=jax.ShapeDtypeStruct((rows, model), jnp.bfloat16),
        grid=(rows // tile,),
        in_specs=[block, pl.BlockSpec((1, model), lambda i: (0, 0))]
        + [pl.BlockSpec(memory_space=pl.ANY)] * len(also),
        out_specs=block,
        compiler_params=pltpu.CompilerParams(vmem_limit_bytes=VMEM_LIMIT),
        cost_estimate=SMALL,
        name="input_norm",
    )(hidden, gain.reshape(1, model), *also)


def project_kernel(index, *refs, count, final, has_acc, heads):
    xs, pieces, rest = refs[:count], refs[count : 2 * count], refs[2 * count :]
    x = jnp.concatenate([ref[...] for ref in xs], axis=1)
    weights = jnp.concatenate([ref[...] for ref in pieces], axis=0)
    total = jnp.dot(x, weights, preferred_element_type=jnp.float32)
    if has_acc:
        total = total + rest[0][...]
        rest = rest[1:]
    if not final:
        rest[0][...] = total
        return
    cos_ref, sin_ref, q_ref, k_ref, v_ref = rest
    cosine, sine = cos_ref[...], sin_ref[...]

    def rotate(u):
        return (u * cosine + pltpu.roll(u, HD // 2, 1) * sine).astype(jnp.bfloat16)

    for h in range(heads):
        q_ref[:, h * HD : (h + 1) * HD] = rotate(total[:, h * HD : (h + 1) * HD])
    key = total[:, heads * HD : (heads + 1) * HD]
    k_ref[...] = rotate(key.astype(jnp.bfloat16).astype(jnp.float32))
    v_ref[...] = total[:, (heads + 1) * HD :].astype(jnp.bfloat16)


def project(index, x, pieces, acc=None, rope=None, also=(), tile=256):
    rows, model = x.shape
    depth, width = pieces[0].shape
    count = len(pieces)
    heads = width // HD - 2
    final = rope is not None
    row_block = lambda w: pl.BlockSpec((tile, w), lambda i, *_: (i, 0))
    in_specs = [
        pl.BlockSpec((tile, depth), lambda i, at, k=k: (i, at[k])) for k in range(count)
    ] + [pl.BlockSpec((depth, width), lambda i, *_: (0, 0), pipeline_mode=pl.Buffered(1))] * count
    args = [x] * count + list(pieces)
    if acc is not None:
        in_specs.append(row_block(width))
        args.append(acc)
    if final:
        in_specs += [row_block(HD)] * 2
        args += list(rope)
        out_shape = [
            jax.ShapeDtypeStruct((rows, heads * HD), jnp.bfloat16),
            jax.ShapeDtypeStruct((rows, HD), jnp.bfloat16),
            jax.ShapeDtypeStruct((rows, HD), jnp.bfloat16),
        ]
        out_specs = [row_block(heads * HD), row_block(HD), row_block(HD)]
    else:
        out_shape = jax.ShapeDtypeStruct((rows, width), jnp.float32)
        out_specs = row_block(width)
    kernel = functools.partial(
        project_kernel, count=count, final=final, has_acc=acc is not None, heads=heads
    )
    kernel = skipping(kernel, 1 + len(args), len(also))
    in_specs += [pl.BlockSpec(memory_space=pl.ANY)] * len(also)
    args += list(also)
    return pl.pallas_call(
        kernel,
        out_shape=out_shape,
        grid_spec=pltpu.PrefetchScalarGridSpec(
            num_scalar_prefetch=1, grid=(rows // tile,), in_specs=in_specs, out_specs=out_specs
        ),
        compiler_params=pltpu.CompilerParams(vmem_limit_bytes=VMEM_LIMIT),
        cost_estimate=SMALL,
        name="project",
    )(index, *args)


def attend_kernel(
    scal, q_ref, k_ref, v_ref, c_ref, *rest, first, heads, tq, tk
):
    o_ref, m_ref, acc_ref = rest[-3:]
    base = first + pl.program_id(0) * tq
    rows = heads * tq
    q = jnp.concatenate([q_ref[:, h * HD : (h + 1) * HD] for h in range(heads)], axis=0)
    m_ref[...] = jnp.full((rows, HD), lowest_peak, jnp.float32)
    acc_ref[...] = jnp.zeros((rows, 2 * HD), jnp.float32)
    token = base + lax.broadcasted_iota(jnp.int32, (tq, 1), 0)
    scale = HD ** (-0.5) * 1.4426950408889634

    def update(keys, values, mask):
        width = keys.shape[0]
        s = lax.dot_general(q, keys, (((1,), (1,)), ((), ())), preferred_element_type=jnp.float32)
        s = s.reshape(heads, tq, width) * scale
        s = jnp.where(mask[None], s, masked_score).reshape(rows, width)
        before = m_ref[...]
        peak = jnp.maximum(before, jnp.max(s, axis=1, keepdims=True))
        m_ref[...] = peak
        keep = jnp.exp2(before - peak)
        p = jnp.exp2(s - jnp.concatenate([peak] * (width // HD), axis=1)).astype(jnp.bfloat16)
        wide = jnp.concatenate([values, jnp.ones((width, HD), jnp.bfloat16)], axis=1)
        acc_ref[...] = acc_ref[...] * jnp.concatenate([keep, keep], axis=1) + jnp.dot(
            p, wide, preferred_element_type=jnp.float32
        )

    for r in range(REQ_REP):
        start, end, pref = scal[r], scal[REQ_REP + r], scal[2 * REQ_REP + r]
        inside = (token >= start) & (token < end)

        @pl.when((start < base + tq) & (end > base))
        def _(r=r, start=start, end=end, pref=pref, inside=inside):
            @pl.loop(0, (pref + tk - 1) // tk)
            def _(j):
                at = pl.ds(pl.multiple_of(r * PREF_MAX + j * tk, tk), tk)
                slot = j * tk + lax.broadcasted_iota(jnp.int32, (1, tk), 1)
                update(c_ref[at, :HD], c_ref[at, HD:], inside & (slot < pref))

            @pl.loop(start // tk, (jnp.minimum(end, base + tq) - 1) // tk + 1)
            def _(j):
                at = pl.ds(pl.multiple_of(j * tk, tk), tk)
                other = j * tk + lax.broadcasted_iota(jnp.int32, (1, tk), 1)
                update(k_ref[at, :], v_ref[at, :], inside & (other >= start) & (other <= token))

    out = (acc_ref[:, :HD] / acc_ref[:, HD:]).astype(jnp.bfloat16)
    for h in range(heads):
        o_ref[:, h * HD : (h + 1) * HD] = out[h * tq : (h + 1) * tq]


def attend(scal, q, k, v, cache, first, rows, earlier=None, also=(), tq=128, tk=256):
    heads = q.shape[1] // HD
    tokens, slots = q.shape[0], cache.shape[0]
    whole = lambda r, w: pl.BlockSpec((r, w), lambda i, *_: (0, 0))
    block = pl.BlockSpec((tq, heads * HD), lambda i, *_: (first // tq + i, 0))
    more = ([] if earlier is None else [earlier]) + list(also)
    return pl.pallas_call(
        functools.partial(attend_kernel, first=first, heads=heads, tq=tq, tk=tk),
        out_shape=jax.ShapeDtypeStruct((tokens, heads * HD), jnp.bfloat16),
        grid_spec=pltpu.PrefetchScalarGridSpec(
            num_scalar_prefetch=1,
            grid=(rows // tq,),
            in_specs=[
                block,
                whole(tokens, HD),
                whole(tokens, HD),
                pl.BlockSpec((slots, 2 * HD), lambda i, s: (0, s[3 * REQ_REP])),
            ]
            + [pl.BlockSpec(memory_space=pl.ANY)] * len(more),
            out_specs=block,
            scratch_shapes=[
                pltpu.VMEM((heads * tq, HD), jnp.float32),
                pltpu.VMEM((heads * tq, 2 * HD), jnp.float32),
            ],
        ),
        input_output_aliases={} if earlier is None else {5: 0},
        compiler_params=pltpu.CompilerParams(vmem_limit_bytes=VMEM_LIMIT),
        cost_estimate=SMALL,
        name="attend",
    )(scal, q, k, v, cache, *more)


def output_kernel(choice, a_ref, *rest, count, slots):
    pieces, outs, (held, sems) = rest[:count], rest[count : count + slots], rest[count + slots :]
    width = outs[0].shape[1]

    @pl.when(pl.program_id(0) == 0)
    def _():
        for s in range(slots):
            for i in range(count):

                @pl.when(choice[s] == i)
                def _(s=s, i=i):
                    pltpu.make_async_copy(
                        pieces[i], held.at[:, pl.ds(s * width, width)], sems.at[s]
                    ).start()

        for s in range(slots):
            pltpu.make_async_copy(
                pieces[0], held.at[:, pl.ds(s * width, width)], sems.at[s]
            ).wait()

    part = jnp.dot(a_ref[...], held[...], preferred_element_type=jnp.float32)
    part = part.astype(jnp.bfloat16)
    for s in range(slots):
        outs[s][...] = part[:, s * width : (s + 1) * width]


def output_parts(choice, attended, pieces, slots, also=(), tile=512):
    rows, depth = attended.shape
    width = pieces[0].shape[1]
    count = len(pieces)
    kernel = functools.partial(output_kernel, count=count, slots=slots)
    return pl.pallas_call(
        skipping(kernel, 2 + count, len(also)),
        out_shape=[jax.ShapeDtypeStruct((rows, width), jnp.bfloat16)] * slots,
        grid_spec=pltpu.PrefetchScalarGridSpec(
            num_scalar_prefetch=1,
            grid=(rows // tile,),
            in_specs=[pl.BlockSpec((tile, depth), lambda i, *_: (i, 0))]
            + [pl.BlockSpec(memory_space=pl.ANY)] * (count + len(also)),
            out_specs=[pl.BlockSpec((tile, width), lambda i, *_: (i, 0))] * slots,
            scratch_shapes=[
                pltpu.VMEM((depth, slots * width), jnp.bfloat16),
                pltpu.SemaphoreType.DMA((slots,)),
            ],
        ),
        compiler_params=pltpu.CompilerParams(vmem_limit_bytes=VMEM_LIMIT),
        cost_estimate=SMALL,
        name="output_parts",
    )(choice, attended, *pieces, *also)


def residual_kernel(where, h_ref, *rest, stages, last):
    terms, rest = rest[: 3 * stages], rest[3 * stages :]
    r_ref, ssq_ref = rest[-2:]
    width = terms[0].shape[1]
    total = rest[1][...] if last else None
    for s in range(stages):
        at = slice(None) if last else pl.ds(pl.multiple_of(where[s] * width, width), width)
        proj = sum(term[...].astype(jnp.float32) for term in terms[3 * s : 3 * s + 3])
        resid = (h_ref[:, at].astype(jnp.float32) + proj).astype(jnp.bfloat16)
        r_ref[:, at] = resid
        wide = resid.astype(jnp.float32)
        square = wide * wide
        for i in range(0, width, HD):
            part = square[:, i : i + HD]
            total = part if total is None else total + part
    if last:
        total = lax.dot_general(
            jnp.ones((8, HD), jnp.float32),
            total,
            (((1,), (1,)), ((), ())),
            precision=lax.Precision.HIGHEST,
            preferred_element_type=jnp.float32,
        )
    ssq_ref[...] = total


def residual(where, hidden, terms, total_width, earlier=None, tile=512):
    rows = hidden.shape[0]
    stages = len(terms)
    terms = [term for stage in terms for term in stage]
    width = terms[0].shape[1]
    last = earlier is not None
    parts = [pl.BlockSpec((tile, width), lambda i, *_: (i, 0))] * len(terms)
    lanes = pl.BlockSpec((tile, HD), lambda i, *_: (i, 0))
    if last:
        in_place = pl.BlockSpec((tile, width), lambda i, w: (i, w[1]))
        out_place = pl.BlockSpec((tile, width), lambda i, w: (i, w[0]))
        more, more_specs = list(earlier), [pl.BlockSpec(memory_space=pl.ANY), lanes]
        aliases = {2 + len(terms): 0}
        ssq_shape, ssq_block = (8, rows), pl.BlockSpec((8, tile), lambda i, *_: (0, i))
    else:
        count = where.shape[0] - 1
        in_place = pl.BlockSpec((tile, total_width), lambda i, w: (i, w[count]))
        out_place = pl.BlockSpec((tile, total_width), lambda i, *_: (i, 0))
        more, more_specs, aliases = [], [], {}
        ssq_shape, ssq_block = (rows, HD), lanes
    return pl.pallas_call(
        functools.partial(residual_kernel, stages=stages, last=last),
        out_shape=[
            jax.ShapeDtypeStruct((rows, total_width), jnp.bfloat16),
            jax.ShapeDtypeStruct(ssq_shape, jnp.float32),
        ],
        grid_spec=pltpu.PrefetchScalarGridSpec(
            num_scalar_prefetch=1,
            grid=(rows // tile,),
            in_specs=[in_place] + parts + more_specs,
            out_specs=[out_place, ssq_block],
        ),
        input_output_aliases=aliases,
        compiler_params=pltpu.CompilerParams(vmem_limit_bytes=VMEM_LIMIT),
        cost_estimate=SMALL,
        name="residual",
    )(where, hidden, *terms, *more)


def output_norm_kernel(*refs, count, model):
    squares, (r_ref, gain_ref, out_ref) = refs[:count], refs[count:]
    total = lax.dot_general(
        jnp.concatenate([ref[...] for ref in squares], axis=0),
        jnp.ones((8 * count, HD), jnp.float32),
        (((0,), (0,)), ((), ())),
        precision=lax.Precision.HIGHEST,
        preferred_element_type=jnp.float32,
    )
    factor = lax.rsqrt(total * (1.0 / (8 * model)) + norm_eps)
    for i in range(0, r_ref.shape[1], HD):
        at = slice(i, i + HD)
        out_ref[:, at] = (r_ref[:, at].astype(jnp.float32) * factor * gain_ref[:, at]).astype(
            jnp.bfloat16
        )


def output_norm(squares, resid, gain, model, tile=512):
    rows, width = resid.shape
    block = pl.BlockSpec((tile, width), lambda i: (i, 0))
    return pl.pallas_call(
        functools.partial(output_norm_kernel, count=len(squares), model=model),
        out_shape=jax.ShapeDtypeStruct((rows, width), jnp.bfloat16),
        grid=(rows // tile,),
        in_specs=[pl.BlockSpec((8, tile), lambda i: (0, i))] * len(squares)
        + [block, pl.BlockSpec((1, width), lambda i: (0, 0))],
        out_specs=block,
        compiler_params=pltpu.CompilerParams(vmem_limit_bytes=VMEM_LIMIT),
        cost_estimate=SMALL,
        name="output_norm",
    )(*squares, resid, gain)


def join_kernel(*refs):
    pass


def join(arrays, *others):
    anywhere = pl.BlockSpec(memory_space=pltpu.HBM)
    count = len(arrays)
    return tuple(
        pl.pallas_call(
            join_kernel,
            out_shape=[jax.ShapeDtypeStruct(p.shape, p.dtype) for p in arrays],
            in_specs=[anywhere] * count + [pl.BlockSpec(memory_space=pl.ANY)] * len(others),
            out_specs=[anywhere] * count,
            input_output_aliases={i: i for i in range(count)},
            compiler_params=pltpu.CompilerParams(vmem_limit_bytes=VMEM_LIMIT),
            cost_estimate=SMALL,
            name="join",
        )(*arrays, *others)
    )


def body(hidden, norm_gain, w_query, w_keyval, w_output, cache, lengths, prefix, out_gain):
    n_rep, n_tp = lax.axis_size("rep"), lax.axis_size("tp")
    rep, tp = lax.axis_index("rep"), lax.axis_index("tp")
    rows, model = hidden.shape
    heads_here = w_query.shape[1] // HD
    order, source, piece, column, last = tables(n_rep, n_tp)
    ahead = [(order[i], order[(i + 1) % n_rep]) for i in range(n_rep)]
    back = [(b, a) for a, b in ahead]
    swap = lambda value, d: lax.ppermute(value, "tp", [(i, i ^ d) for i in range(n_tp)])
    step = lambda pair: (lax.ppermute(pair[0], "rep", ahead), lax.ppermute(pair[1], "rep", back))

    mid = w_output.shape[1] // 2
    out_pairs = [(w_output[:, :mid], w_output[:, mid:])]
    out_pairs.append(step(out_pairs[0]))

    kv_head_of = lambda t: t * heads_here // (H // KV)
    feats = w_keyval.shape[1] // KV
    col = jnp.arange(w_keyval.shape[1], dtype=jnp.int32)[:, None]
    feat = jnp.arange(feats, dtype=jnp.int32)[None, :]
    parts = []
    for d in range(n_tp):
        pick = (col == feat * KV + kv_head_of(tp ^ d)).astype(jnp.bfloat16)
        mine = jnp.dot(w_keyval, pick, preferred_element_type=jnp.float32).astype(jnp.bfloat16)
        parts.append(swap(mine, d) if d else mine)
    mixed = jnp.concatenate(parts, axis=1)
    slot = jnp.arange(mixed.shape[1], dtype=jnp.int32)
    home = ((slot // feats) ^ tp) * feats + slot % feats
    place = (home[:, None] == slot[None, :]).astype(jnp.bfloat16)
    keyval = jnp.dot(mixed, place, preferred_element_type=jnp.float32).astype(jnp.bfloat16)

    joined = jnp.concatenate([w_query, keyval], axis=1)
    depth = joined.shape[0] // 2

    lens = lengths.reshape(-1)
    position, starts, ends = request_position(lens, prefix, rows)
    rope = rope_tables(position)
    scal = jnp.concatenate(
        [starts, ends, prefix, kv_head_of(tp).astype(jnp.int32)[None]]
    ).astype(jnp.int32)

    bits = n_tp.bit_length() - 1
    dests = tp ^ jnp.asarray([bit_reverse(s, bits) for s in range(n_tp)], jnp.int32)
    choice_all = jnp.asarray(piece)[rep][dests]
    column_all = jnp.asarray(column)[rep][tp]
    halves = piece.shape[2]
    choices = [choice_all[:, s] for s in range(halves)]
    where_early = jnp.concatenate([column_all[:-1], tp[None]]).astype(jnp.int32)
    where_last = jnp.stack([column_all[-1], tp * halves + column_all[-1]]).astype(jnp.int32)
    width = model // n_tp
    gain = lax.dynamic_slice_in_dim(out_gain, tp * width, width, 0).astype(jnp.float32).reshape(1, width)

    first_cut, second_cut = n_rep // 2, n_rep - 2
    index = jnp.asarray(source)[rep]
    cuts = [0, first_cut, second_cut, n_rep]
    indices = [index[2 * low : 2 * high] for low, high in zip(cuts[:-1], cuts[1:])]
    in_pairs = [join((joined[:depth], joined[depth:]), *out_pairs[1])]
    x = input_norm(hidden, norm_gain, in_pairs[0][:1])
    acc, done = None, 0

    def project_arrived(acc, done, rope=None, also=()):
        ready = [p for pair in in_pairs[done:] for p in pair]
        return project(indices[cuts.index(done)], x, ready, acc, rope, also)

    for k in range(1, n_rep):
        arrived = step(in_pairs[-1])
        if k == 2:
            arrived = join(arrived, x)
        if k == 3:
            arrived = join(
                arrived, scal, *rope, *choices, where_early, where_last, gain, *indices
            )
        if k in (first_cut, second_cut):
            acc, done = project_arrived(acc, done), k
            arrived = join(arrived, acc)
        in_pairs.append(arrived)

    out_pairs[1] = join(out_pairs[1], *in_pairs[-1])
    q, k, v = project_arrived(acc, done, rope, out_pairs[1][:1])

    def stage(members, attended, also=()):
        pieces = [p for pair in out_pairs[: last[members[-1]] + 1] for p in pair]
        choice = jnp.stack([choices[s] for s in members], axis=1).reshape(-1)
        return output_parts(choice, attended, pieces, choice.shape[0], also)

    def exchange(parts, count):
        d = 1
        while True:
            half = len(parts) // 2
            received = [swap(part, d) for part in parts[half:]]
            pairs = list(zip(parts[:half], received))
            if half == 2 * count:
                return pairs[:count], pairs[count:]
            parts, d = [add(*pair) for pair in pairs], d * 2

    def add(a, b):
        return (a.astype(jnp.float32) + b.astype(jnp.float32)).astype(jnp.bfloat16)

    terms = []

    def collect(parts, cut=None):
        spans = [slice(0, rows)] if cut is None else [slice(0, cut), slice(cut, rows)]
        all_sends, all_recvs = [], []
        for stay, leave in zip(*exchange(parts, len(parts) // n_tp)):
            sends = [add(*(a[span] for a in leave)) for span in spans]
            recvs = [swap(part, n_tp // 2) for part in sends]
            terms.append((*stay, recvs[0] if cut is None else jnp.concatenate(recvs, axis=0)))
            all_sends += sends
            all_recvs += recvs
        return all_sends, all_recvs

    shares = [0, 1, 4, 7, 8]
    tq = rows // shares[-1]
    attended, raw, sent, pending = None, None, [], [[s] for s in range(halves)]
    if halves > 3:
        pending[:2] = [[0, 1]]
    for flight in range(2, n_rep):
        arrived = step(out_pairs[-1])
        own = list(out_pairs[-1][:1])
        waits = []
        if flight - 2 < len(shares) - 1:
            low, high = shares[flight - 2 : flight]
            attended = attend(
                scal, q, k, v, cache, low * tq, (high - low) * tq, attended, own, tq=tq
            )
            waits = [attended]
        if flight >= len(shares):
            gates = [*own, *sent[:1]]
            waits += sent[1:]
            sent = []
            if raw is not None:
                sends, sent = collect(raw)
                waits, raw = waits + sends, None
            elif last[pending[0][-1]] < flight and len(pending) > 1:
                raw = stage(pending.pop(0), attended, gates)
                half = len(raw) // 2
                arrived = join((*arrived, *raw[half:]), *waits)
                raw, arrived, waits = [*raw[:half], *arrived[2:]], arrived[:2], []
        out_pairs.append(join(arrived, *waits) if waits else tuple(arrived))

    recvs = []
    while pending:
        gates = []
        if raw is not None:
            gates, recvs = collect(raw, rows * 3 // 4)
        raw = stage(pending.pop(0), attended, gates)
    early = residual(where_early, hidden, terms, width)
    half = len(raw) // 2
    raw = [*raw[:half], *join(raw[half:], *recvs[:1])]
    collect(raw)
    resid, ssq = residual(where_last, hidden, terms[-1:], width, early)

    squares = [ssq] + [swap(ssq, d) for d in range(1, n_tp)]
    normed = output_norm(squares, resid, gain, model)
    return (resid, normed)


def solution(mesh):
    placed = (
        P("rep", None),
        P(),
        P("rep", "tp"),
        P("rep", "tp"),
        P("tp", "rep"),
        P("rep", None),
        P("rep", None),
        P("rep"),
        P(),
    )
    return jax.shard_map(
        body,
        mesh=mesh,
        in_specs=placed,
        out_specs=(P("rep", "tp"), P("rep", "tp")),
        check_vma=False,
    )
```

```python
import functools

import jax
import jax.numpy as jnp
import numpy as np
from jax import lax
from jax.experimental import pallas as pl
from jax.experimental.pallas import tpu as pltpu
from jax.sharding import PartitionSpec as P

H = 32
KV = 4
HD = 128
REQ_REP = 4
PREF_MAX = 512

norm_eps = 1e-05
rope_base = 5000000.0
masked_score = -1e30
lowest_peak = -1e25

VMEM_LIMIT = 63 * 1024 * 1024

SMALL = pl.CostEstimate(flops=1024, bytes_accessed=1024, transcendentals=0)


def ring_order(count):
    return list(range(0, count, 2)) + list(range(count - 1, 0, -2))


def bit_reverse(value, bits):
    return sum(((value >> b) & 1) << (bits - 1 - b) for b in range(bits))


def tables(n_rep, n_tp):
    order = ring_order(n_rep)
    place = [order.index(r) for r in range(n_rep)]
    halves = 2 * n_rep // n_tp
    source = np.zeros((n_rep, 2 * n_rep), np.int32)
    piece = np.zeros((n_rep, n_tp, halves), np.int32)
    column = np.zeros((n_rep, n_tp, halves), np.int32)
    last = [0] * halves
    for r in range(n_rep):
        seen = [0] * n_tp
        for k in range(n_rep):
            for h, src in ((0, order[(place[r] - k) % n_rep]), (1, order[(place[r] + k) % n_rep])):
                source[r, 2 * k + h] = src * 2 + h
                dest = src * n_tp // n_rep
                s = seen[dest]
                seen[dest] += 1
                piece[r, dest, s] = 2 * k + h
                column[r, dest, s] = src * 2 + h - dest * halves
                last[s] = max(last[s], k)
    return order, source, piece, column, last


def rope_tables(position):
    half = HD // 2
    freqs = rope_base ** (-(jnp.arange(half, dtype=jnp.float32) * 2.0 / HD))
    angles = position.astype(jnp.float32)[:, None] * freqs[None, :]
    cosine, sine = jnp.cos(angles), jnp.sin(angles)
    return jnp.concatenate([cosine, cosine], 1), jnp.concatenate([-sine, sine], 1)


def request_position(lens, prefs, count):
    token_ids = jnp.arange(count, dtype=jnp.int32)
    ends = jnp.cumsum(lens)
    starts = ends - lens
    segment = jnp.sum((token_ids[:, None] >= ends[None, :]).astype(jnp.int32), axis=1)
    onehot = segment[:, None] == jnp.arange(lens.shape[0], dtype=jnp.int32)[None, :]
    shift = jnp.sum(jnp.where(onehot, (prefs - starts)[None, :], 0), axis=1)
    return token_ids + shift, starts, ends


def skipping(kernel, first, count):
    return lambda *refs: kernel(*refs[:first], *refs[first + count :])


def norm_kernel(h_ref, gain_ref, *rest):
    out_ref = rest[-1]
    values = h_ref[...].astype(jnp.float32)
    meansq = jnp.mean(values * values, axis=-1, keepdims=True)
    gain = gain_ref[...].astype(jnp.float32)
    out_ref[...] = (values * lax.rsqrt(meansq + norm_eps) * gain).astype(jnp.bfloat16)


def input_norm(hidden, gain, also, tile=128):
    rows, model = hidden.shape
    block = pl.BlockSpec((tile, model), lambda i: (i, 0))
    return pl.pallas_call(
        norm_kernel,
        out_shape=jax.ShapeDtypeStruct((rows, model), jnp.bfloat16),
        grid=(rows // tile,),
        in_specs=[block, pl.BlockSpec((1, model), lambda i: (0, 0))]
        + [pl.BlockSpec(memory_space=pl.ANY)] * len(also),
        out_specs=block,
        compiler_params=pltpu.CompilerParams(vmem_limit_bytes=VMEM_LIMIT),
        cost_estimate=SMALL,
        name="input_norm",
    )(hidden, gain.reshape(1, model), *also)


def project_kernel(index, *refs, count, final, has_acc, heads):
    xs, pieces, rest = refs[:count], refs[count : 2 * count], refs[2 * count :]
    x = jnp.concatenate([ref[...] for ref in xs], axis=1)
    weights = jnp.concatenate([ref[...] for ref in pieces], axis=0)
    total = jnp.dot(x, weights, preferred_element_type=jnp.float32)
    if has_acc:
        total = total + rest[0][...]
        rest = rest[1:]
    if not final:
        rest[0][...] = total
        return
    cos_ref, sin_ref, q_ref, k_ref, v_ref = rest
    cosine, sine = cos_ref[...], sin_ref[...]

    def rotate(u):
        return (u * cosine + pltpu.roll(u, HD // 2, 1) * sine).astype(jnp.bfloat16)

    for h in range(heads):
        q_ref[:, h * HD : (h + 1) * HD] = rotate(total[:, h * HD : (h + 1) * HD])
    key = total[:, heads * HD : (heads + 1) * HD]
    k_ref[...] = rotate(key.astype(jnp.bfloat16).astype(jnp.float32))
    v_ref[...] = total[:, (heads + 1) * HD :].astype(jnp.bfloat16)


def project(index, x, pieces, acc=None, rope=None, also=(), tile=256):
    rows, model = x.shape
    depth, width = pieces[0].shape
    count = len(pieces)
    heads = width // HD - 2
    final = rope is not None
    row_block = lambda w: pl.BlockSpec((tile, w), lambda i, *_: (i, 0))
    in_specs = [
        pl.BlockSpec((tile, depth), lambda i, at, k=k: (i, at[k])) for k in range(count)
    ] + [pl.BlockSpec((depth, width), lambda i, *_: (0, 0), pipeline_mode=pl.Buffered(1))] * count
    args = [x] * count + list(pieces)
    if acc is not None:
        in_specs.append(row_block(width))
        args.append(acc)
    if final:
        in_specs += [row_block(HD)] * 2
        args += list(rope)
        out_shape = [
            jax.ShapeDtypeStruct((rows, heads * HD), jnp.bfloat16),
            jax.ShapeDtypeStruct((rows, HD), jnp.bfloat16),
            jax.ShapeDtypeStruct((rows, HD), jnp.bfloat16),
        ]
        out_specs = [row_block(heads * HD), row_block(HD), row_block(HD)]
    else:
        out_shape = jax.ShapeDtypeStruct((rows, width), jnp.float32)
        out_specs = row_block(width)
    kernel = functools.partial(
        project_kernel, count=count, final=final, has_acc=acc is not None, heads=heads
    )
    kernel = skipping(kernel, 1 + len(args), len(also))
    in_specs += [pl.BlockSpec(memory_space=pl.ANY)] * len(also)
    args += list(also)
    return pl.pallas_call(
        kernel,
        out_shape=out_shape,
        grid_spec=pltpu.PrefetchScalarGridSpec(
            num_scalar_prefetch=1, grid=(rows // tile,), in_specs=in_specs, out_specs=out_specs
        ),
        compiler_params=pltpu.CompilerParams(vmem_limit_bytes=VMEM_LIMIT),
        cost_estimate=SMALL,
        name="project",
    )(index, *args)


def attend_kernel(
    scal, q_ref, k_ref, v_ref, c_ref, *rest, first, heads, tq, tk
):
    o_ref, m_ref, acc_ref = rest[-3:]
    base = first + pl.program_id(0) * tq
    rows = heads * tq
    q = jnp.concatenate([q_ref[:, h * HD : (h + 1) * HD] for h in range(heads)], axis=0)
    m_ref[...] = jnp.full((rows, HD), lowest_peak, jnp.float32)
    acc_ref[...] = jnp.zeros((rows, 2 * HD), jnp.float32)
    token = base + lax.broadcasted_iota(jnp.int32, (tq, 1), 0)
    scale = HD ** (-0.5) * 1.4426950408889634

    def update(keys, values, mask):
        width = keys.shape[0]
        s = lax.dot_general(q, keys, (((1,), (1,)), ((), ())), preferred_element_type=jnp.float32)
        s = s.reshape(heads, tq, width) * scale
        s = jnp.where(mask[None], s, masked_score).reshape(rows, width)
        before = m_ref[...]
        peak = jnp.maximum(before, jnp.max(s, axis=1, keepdims=True))
        m_ref[...] = peak
        keep = jnp.exp2(before - peak)
        p = jnp.exp2(s - jnp.concatenate([peak] * (width // HD), axis=1)).astype(jnp.bfloat16)
        wide = jnp.concatenate([values, jnp.ones((width, HD), jnp.bfloat16)], axis=1)
        acc_ref[...] = acc_ref[...] * jnp.concatenate([keep, keep], axis=1) + jnp.dot(
            p, wide, preferred_element_type=jnp.float32
        )

    for r in range(REQ_REP):
        start, end, pref = scal[r], scal[REQ_REP + r], scal[2 * REQ_REP + r]
        inside = (token >= start) & (token < end)

        @pl.when((start < base + tq) & (end > base))
        def _(r=r, start=start, end=end, pref=pref, inside=inside):
            @pl.loop(0, (pref + tk - 1) // tk)
            def _(j):
                at = pl.ds(pl.multiple_of(r * PREF_MAX + j * tk, tk), tk)
                slot = j * tk + lax.broadcasted_iota(jnp.int32, (1, tk), 1)
                update(c_ref[at, :HD], c_ref[at, HD:], inside & (slot < pref))

            @pl.loop(start // tk, (jnp.minimum(end, base + tq) - 1) // tk + 1)
            def _(j):
                at = pl.ds(pl.multiple_of(j * tk, tk), tk)
                other = j * tk + lax.broadcasted_iota(jnp.int32, (1, tk), 1)
                update(k_ref[at, :], v_ref[at, :], inside & (other >= start) & (other <= token))

    out = (acc_ref[:, :HD] / acc_ref[:, HD:]).astype(jnp.bfloat16)
    for h in range(heads):
        o_ref[:, h * HD : (h + 1) * HD] = out[h * tq : (h + 1) * tq]


def attend(scal, q, k, v, cache, first, rows, earlier=None, also=(), tq=128, tk=256):
    heads = q.shape[1] // HD
    tokens, slots = q.shape[0], cache.shape[0]
    whole = lambda r, w: pl.BlockSpec((r, w), lambda i, *_: (0, 0))
    block = pl.BlockSpec((tq, heads * HD), lambda i, *_: (first // tq + i, 0))
    more = ([] if earlier is None else [earlier]) + list(also)
    return pl.pallas_call(
        functools.partial(attend_kernel, first=first, heads=heads, tq=tq, tk=tk),
        out_shape=jax.ShapeDtypeStruct((tokens, heads * HD), jnp.bfloat16),
        grid_spec=pltpu.PrefetchScalarGridSpec(
            num_scalar_prefetch=1,
            grid=(rows // tq,),
            in_specs=[
                block,
                whole(tokens, HD),
                whole(tokens, HD),
                pl.BlockSpec((slots, 2 * HD), lambda i, s: (0, s[3 * REQ_REP])),
            ]
            + [pl.BlockSpec(memory_space=pl.ANY)] * len(more),
            out_specs=block,
            scratch_shapes=[
                pltpu.VMEM((heads * tq, HD), jnp.float32),
                pltpu.VMEM((heads * tq, 2 * HD), jnp.float32),
            ],
        ),
        input_output_aliases={} if earlier is None else {5: 0},
        compiler_params=pltpu.CompilerParams(vmem_limit_bytes=VMEM_LIMIT),
        cost_estimate=SMALL,
        name="attend",
    )(scal, q, k, v, cache, *more)


def output_kernel(choice, a_ref, *rest, count, slots):
    pieces, outs, (held, sems) = rest[:count], rest[count : count + slots], rest[count + slots :]
    width = outs[0].shape[1]

    @pl.when(pl.program_id(0) == 0)
    def _():
        for s in range(slots):
            for i in range(count):

                @pl.when(choice[s] == i)
                def _(s=s, i=i):
                    pltpu.make_async_copy(
                        pieces[i], held.at[:, pl.ds(s * width, width)], sems.at[s]
                    ).start()

        for s in range(slots):
            pltpu.make_async_copy(
                pieces[0], held.at[:, pl.ds(s * width, width)], sems.at[s]
            ).wait()

    part = jnp.dot(a_ref[...], held[...], preferred_element_type=jnp.float32)
    part = part.astype(jnp.bfloat16)
    for s in range(slots):
        outs[s][...] = part[:, s * width : (s + 1) * width]


def output_parts(choice, attended, pieces, slots, also=(), tile=512):
    rows, depth = attended.shape
    width = pieces[0].shape[1]
    count = len(pieces)
    kernel = functools.partial(output_kernel, count=count, slots=slots)
    return pl.pallas_call(
        skipping(kernel, 2 + count, len(also)),
        out_shape=[jax.ShapeDtypeStruct((rows, width), jnp.bfloat16)] * slots,
        grid_spec=pltpu.PrefetchScalarGridSpec(
            num_scalar_prefetch=1,
            grid=(rows // tile,),
            in_specs=[pl.BlockSpec((tile, depth), lambda i, *_: (i, 0))]
            + [pl.BlockSpec(memory_space=pl.ANY)] * (count + len(also)),
            out_specs=[pl.BlockSpec((tile, width), lambda i, *_: (i, 0))] * slots,
            scratch_shapes=[
                pltpu.VMEM((depth, slots * width), jnp.bfloat16),
                pltpu.SemaphoreType.DMA((slots,)),
            ],
        ),
        compiler_params=pltpu.CompilerParams(vmem_limit_bytes=VMEM_LIMIT),
        cost_estimate=SMALL,
        name="output_parts",
    )(choice, attended, *pieces, *also)


def residual_kernel(where, h_ref, *rest, stages, last):
    terms, rest = rest[: 3 * stages], rest[3 * stages :]
    r_ref, ssq_ref = rest[-2:]
    width = terms[0].shape[1]
    total = rest[1][...] if last else None
    for s in range(stages):
        at = slice(None) if last else pl.ds(pl.multiple_of(where[s] * width, width), width)
        proj = sum(term[...].astype(jnp.float32) for term in terms[3 * s : 3 * s + 3])
        resid = (h_ref[:, at].astype(jnp.float32) + proj).astype(jnp.bfloat16)
        r_ref[:, at] = resid
        wide = resid.astype(jnp.float32)
        square = wide * wide
        for i in range(0, width, HD):
            part = square[:, i : i + HD]
            total = part if total is None else total + part
    if last:
        total = lax.dot_general(
            jnp.ones((8, HD), jnp.float32),
            total,
            (((1,), (1,)), ((), ())),
            precision=lax.Precision.HIGHEST,
            preferred_element_type=jnp.float32,
        )
    ssq_ref[...] = total


def residual(where, hidden, terms, total_width, earlier=None, tile=512):
    rows = hidden.shape[0]
    stages = len(terms)
    terms = [term for stage in terms for term in stage]
    width = terms[0].shape[1]
    last = earlier is not None
    parts = [pl.BlockSpec((tile, width), lambda i, *_: (i, 0))] * len(terms)
    lanes = pl.BlockSpec((tile, HD), lambda i, *_: (i, 0))
    if last:
        in_place = pl.BlockSpec((tile, width), lambda i, w: (i, w[1]))
        out_place = pl.BlockSpec((tile, width), lambda i, w: (i, w[0]))
        more, more_specs = list(earlier), [pl.BlockSpec(memory_space=pl.ANY), lanes]
        aliases = {2 + len(terms): 0}
        ssq_shape, ssq_block = (8, rows), pl.BlockSpec((8, tile), lambda i, *_: (0, i))
    else:
        count = where.shape[0] - 1
        in_place = pl.BlockSpec((tile, total_width), lambda i, w: (i, w[count]))
        out_place = pl.BlockSpec((tile, total_width), lambda i, *_: (i, 0))
        more, more_specs, aliases = [], [], {}
        ssq_shape, ssq_block = (rows, HD), lanes
    return pl.pallas_call(
        functools.partial(residual_kernel, stages=stages, last=last),
        out_shape=[
            jax.ShapeDtypeStruct((rows, total_width), jnp.bfloat16),
            jax.ShapeDtypeStruct(ssq_shape, jnp.float32),
        ],
        grid_spec=pltpu.PrefetchScalarGridSpec(
            num_scalar_prefetch=1,
            grid=(rows // tile,),
            in_specs=[in_place] + parts + more_specs,
            out_specs=[out_place, ssq_block],
        ),
        input_output_aliases=aliases,
        compiler_params=pltpu.CompilerParams(vmem_limit_bytes=VMEM_LIMIT),
        cost_estimate=SMALL,
        name="residual",
    )(where, hidden, *terms, *more)


def output_norm_kernel(*refs, count, model):
    squares, (r_ref, gain_ref, out_ref) = refs[:count], refs[count:]
    total = lax.dot_general(
        jnp.concatenate([ref[...] for ref in squares], axis=0),
        jnp.ones((8 * count, HD), jnp.float32),
        (((0,), (0,)), ((), ())),
        precision=lax.Precision.HIGHEST,
        preferred_element_type=jnp.float32,
    )
    factor = lax.rsqrt(total * (1.0 / (8 * model)) + norm_eps)
    for i in range(0, r_ref.shape[1], HD):
        at = slice(i, i + HD)
        out_ref[:, at] = (r_ref[:, at].astype(jnp.float32) * factor * gain_ref[:, at]).astype(
            jnp.bfloat16
        )


def output_norm(squares, resid, gain, model, tile=512):
    rows, width = resid.shape
    block = pl.BlockSpec((tile, width), lambda i: (i, 0))
    return pl.pallas_call(
        functools.partial(output_norm_kernel, count=len(squares), model=model),
        out_shape=jax.ShapeDtypeStruct((rows, width), jnp.bfloat16),
        grid=(rows // tile,),
        in_specs=[pl.BlockSpec((8, tile), lambda i: (0, i))] * len(squares)
        + [block, pl.BlockSpec((1, width), lambda i: (0, 0))],
        out_specs=block,
        compiler_params=pltpu.CompilerParams(vmem_limit_bytes=VMEM_LIMIT),
        cost_estimate=SMALL,
        name="output_norm",
    )(*squares, resid, gain)


def join_kernel(*refs):
    pass


def join(arrays, *others):
    anywhere = pl.BlockSpec(memory_space=pltpu.HBM)
    count = len(arrays)
    return tuple(
        pl.pallas_call(
            join_kernel,
            out_shape=[jax.ShapeDtypeStruct(p.shape, p.dtype) for p in arrays],
            in_specs=[anywhere] * count + [pl.BlockSpec(memory_space=pl.ANY)] * len(others),
            out_specs=[anywhere] * count,
            input_output_aliases={i: i for i in range(count)},
            compiler_params=pltpu.CompilerParams(vmem_limit_bytes=VMEM_LIMIT),
            cost_estimate=SMALL,
            name="join",
        )(*arrays, *others)
    )


def body(hidden, norm_gain, w_query, w_keyval, w_output, cache, lengths, prefix, out_gain):
    n_rep, n_tp = lax.axis_size("rep"), lax.axis_size("tp")
    rep, tp = lax.axis_index("rep"), lax.axis_index("tp")
    rows, model = hidden.shape
    heads_here = w_query.shape[1] // HD
    order, source, piece, column, last = tables(n_rep, n_tp)
    ahead = [(order[i], order[(i + 1) % n_rep]) for i in range(n_rep)]
    back = [(b, a) for a, b in ahead]
    swap = lambda value, d: lax.ppermute(value, "tp", [(i, i ^ d) for i in range(n_tp)])
    step = lambda pair: (lax.ppermute(pair[0], "rep", ahead), lax.ppermute(pair[1], "rep", back))

    mid = w_output.shape[1] // 2
    out_pairs = [(w_output[:, :mid], w_output[:, mid:])]
    out_pairs.append(step(out_pairs[0]))

    kv_head_of = lambda t: t * heads_here // (H // KV)
    feats = w_keyval.shape[1] // KV
    col = jnp.arange(w_keyval.shape[1], dtype=jnp.int32)[:, None]
    feat = jnp.arange(feats, dtype=jnp.int32)[None, :]
    parts = []
    for d in range(n_tp):
        pick = (col == feat * KV + kv_head_of(tp ^ d)).astype(jnp.bfloat16)
        mine = jnp.dot(w_keyval, pick, preferred_element_type=jnp.float32).astype(jnp.bfloat16)
        parts.append(swap(mine, d) if d else mine)
    mixed = jnp.concatenate(parts, axis=1)
    slot = jnp.arange(mixed.shape[1], dtype=jnp.int32)
    home = ((slot // feats) ^ tp) * feats + slot % feats
    place = (home[:, None] == slot[None, :]).astype(jnp.bfloat16)
    keyval = jnp.dot(mixed, place, preferred_element_type=jnp.float32).astype(jnp.bfloat16)

    joined = jnp.concatenate([w_query, keyval], axis=1)
    depth = joined.shape[0] // 2

    lens = lengths.reshape(-1)
    position, starts, ends = request_position(lens, prefix, rows)
    rope = rope_tables(position)
    scal = jnp.concatenate(
        [starts, ends, prefix, kv_head_of(tp).astype(jnp.int32)[None]]
    ).astype(jnp.int32)

    bits = n_tp.bit_length() - 1
    dests = tp ^ jnp.asarray([bit_reverse(s, bits) for s in range(n_tp)], jnp.int32)
    choice_all = jnp.asarray(piece)[rep][dests]
    column_all = jnp.asarray(column)[rep][tp]
    halves = piece.shape[2]
    choices = [choice_all[:, s] for s in range(halves)]
    where_early = jnp.concatenate([column_all[:-1], tp[None]]).astype(jnp.int32)
    where_last = jnp.stack([column_all[-1], tp * halves + column_all[-1]]).astype(jnp.int32)
    width = model // n_tp
    gain = lax.dynamic_slice_in_dim(out_gain, tp * width, width, 0).astype(jnp.float32).reshape(1, width)

    first_cut, second_cut = n_rep // 2, n_rep - 2
    index = jnp.asarray(source)[rep]
    cuts = [0, first_cut, second_cut, n_rep]
    indices = [index[2 * low : 2 * high] for low, high in zip(cuts[:-1], cuts[1:])]
    in_pairs = [join((joined[:depth], joined[depth:]), *out_pairs[1])]
    x = input_norm(hidden, norm_gain, in_pairs[0][:1])
    acc, done = None, 0

    def project_arrived(acc, done, rope=None, also=()):
        ready = [p for pair in in_pairs[done:] for p in pair]
        return project(indices[cuts.index(done)], x, ready, acc, rope, also)

    for k in range(1, n_rep):
        arrived = step(in_pairs[-1])
        if k == 2:
            arrived = join(arrived, x)
        if k == 3:
            arrived = join(
                arrived, scal, *rope, *choices, where_early, where_last, gain, *indices
            )
        if k in (first_cut, second_cut):
            acc, done = project_arrived(acc, done), k
            arrived = join(arrived, acc)
        in_pairs.append(arrived)

    out_pairs[1] = join(out_pairs[1], *in_pairs[-1])
    q, k, v = project_arrived(acc, done, rope, out_pairs[1][:1])

    def stage(members, attended, also=()):
        pieces = [p for pair in out_pairs[: last[members[-1]] + 1] for p in pair]
        choice = jnp.stack([choices[s] for s in members], axis=1).reshape(-1)
        return output_parts(choice, attended, pieces, choice.shape[0], also)

    def exchange(parts, count):
        d = 1
        while True:
            half = len(parts) // 2
            received = [swap(part, d) for part in parts[half:]]
            pairs = list(zip(parts[:half], received))
            if half == 2 * count:
                return pairs[:count], pairs[count:]
            parts, d = [add(*pair) for pair in pairs], d * 2

    def add(a, b):
        return (a.astype(jnp.float32) + b.astype(jnp.float32)).astype(jnp.bfloat16)

    terms = []

    def collect(parts, cut=None):
        spans = [slice(0, rows)] if cut is None else [slice(0, cut), slice(cut, rows)]
        all_sends, all_recvs = [], []
        for stay, leave in zip(*exchange(parts, len(parts) // n_tp)):
            sends = [add(*(a[span] for a in leave)) for span in spans]
            recvs = [swap(part, n_tp // 2) for part in sends]
            terms.append((*stay, recvs[0] if cut is None else jnp.concatenate(recvs, axis=0)))
            all_sends += sends
            all_recvs += recvs
        return all_sends, all_recvs

    shares = [0, 3, 6, 8]
    tq = rows // shares[-1]
    attended, raw, sent, pending = None, None, [], [[s] for s in range(halves)]
    if halves > 3:
        pending[:2] = [[0, 1]]
    for flight in range(2, n_rep):
        arrived = step(out_pairs[-1])
        own = list(out_pairs[-1][:1])
        waits = []
        if flight == 2:
            waits = [q]
        elif flight - 3 < len(shares) - 1:
            low, high = shares[flight - 3 : flight - 1]
            attended = attend(
                scal, q, k, v, cache, low * tq, (high - low) * tq, attended, own, tq=tq
            )
            waits = [attended]
        if flight > len(shares):
            gates = [*own, *sent[:1]]
            waits += sent[1:]
            sent = []
            if raw is not None:
                sends, sent = collect(raw)
                waits, raw = waits + sends, None
            elif last[pending[0][-1]] < flight and len(pending) > 1:
                raw = stage(pending.pop(0), attended, gates)
                half = len(raw) // 2
                arrived = join((*arrived, *raw[half:]), *waits)
                raw, arrived, waits = [*raw[:half], *arrived[2:]], arrived[:2], []
        out_pairs.append(join(arrived, *waits) if waits else tuple(arrived))

    recvs = []
    while pending:
        gates = []
        if raw is not None:
            gates, recvs = collect(raw, rows * 3 // 4)
        raw = stage(pending.pop(0), attended, gates)
    early = residual(where_early, hidden, terms, width)
    half = len(raw) // 2
    raw = [*raw[:half], *join(raw[half:], *recvs[:1])]
    collect(raw)
    resid, ssq = residual(where_last, hidden, terms[-1:], width, early)

    squares = [ssq] + [swap(ssq, d) for d in range(1, n_tp)]
    normed = output_norm(squares, resid, gain, model)
    return (resid, normed)


def solution(mesh):
    placed = (
        P("rep", None),
        P(),
        P("rep", "tp"),
        P("rep", "tp"),
        P("tp", "rep"),
        P("rep", None),
        P("rep", None),
        P("rep"),
        P(),
    )
    return jax.shard_map(
        body,
        mesh=mesh,
        in_specs=placed,
        out_specs=(P("rep", "tp"), P("rep", "tp")),
        check_vma=False,
    )
```

```python
import functools

import jax
import jax.numpy as jnp
import numpy as np
from jax import lax
from jax.experimental import pallas as pl
from jax.experimental.pallas import tpu as pltpu
from jax.sharding import PartitionSpec as P

H = 32
KV = 4
HD = 128
REQ_REP = 4
PREF_MAX = 512

norm_eps = 1e-05
rope_base = 5000000.0
masked_score = -1e30
lowest_peak = -1e25

VMEM_LIMIT = 63 * 1024 * 1024

SMALL = pl.CostEstimate(flops=1024, bytes_accessed=1024, transcendentals=0)


def ring_order(count):
    return list(range(0, count, 2)) + list(range(count - 1, 0, -2))


def bit_reverse(value, bits):
    return sum(((value >> b) & 1) << (bits - 1 - b) for b in range(bits))


def tables(n_rep, n_tp):
    order = ring_order(n_rep)
    place = [order.index(r) for r in range(n_rep)]
    halves = 2 * n_rep // n_tp
    source = np.zeros((n_rep, 2 * n_rep), np.int32)
    piece = np.zeros((n_rep, n_tp, halves), np.int32)
    column = np.zeros((n_rep, n_tp, halves), np.int32)
    last = [0] * halves
    for r in range(n_rep):
        seen = [0] * n_tp
        for k in range(n_rep):
            for h, src in ((0, order[(place[r] - k) % n_rep]), (1, order[(place[r] + k) % n_rep])):
                source[r, 2 * k + h] = src * 2 + h
                dest = src * n_tp // n_rep
                s = seen[dest]
                seen[dest] += 1
                piece[r, dest, s] = 2 * k + h
                column[r, dest, s] = src * 2 + h - dest * halves
                last[s] = max(last[s], k)
    return order, source, piece, column, last


def rope_tables(position):
    half = HD // 2
    freqs = rope_base ** (-(jnp.arange(half, dtype=jnp.float32) * 2.0 / HD))
    angles = position.astype(jnp.float32)[:, None] * freqs[None, :]
    cosine, sine = jnp.cos(angles), jnp.sin(angles)
    return jnp.concatenate([cosine, cosine], 1), jnp.concatenate([-sine, sine], 1)


def request_position(lens, prefs, count):
    token_ids = jnp.arange(count, dtype=jnp.int32)
    ends = jnp.cumsum(lens)
    starts = ends - lens
    segment = jnp.sum((token_ids[:, None] >= ends[None, :]).astype(jnp.int32), axis=1)
    onehot = segment[:, None] == jnp.arange(lens.shape[0], dtype=jnp.int32)[None, :]
    shift = jnp.sum(jnp.where(onehot, (prefs - starts)[None, :], 0), axis=1)
    return token_ids + shift, starts, ends


def skipping(kernel, first, count):
    return lambda *refs: kernel(*refs[:first], *refs[first + count :])


def norm_kernel(h_ref, gain_ref, *rest):
    out_ref = rest[-1]
    values = h_ref[...].astype(jnp.float32)
    meansq = jnp.mean(values * values, axis=-1, keepdims=True)
    gain = gain_ref[...].astype(jnp.float32)
    out_ref[...] = (values * lax.rsqrt(meansq + norm_eps) * gain).astype(jnp.bfloat16)


def input_norm(hidden, gain, also, tile=128):
    rows, model = hidden.shape
    block = pl.BlockSpec((tile, model), lambda i: (i, 0))
    return pl.pallas_call(
        norm_kernel,
        out_shape=jax.ShapeDtypeStruct((rows, model), jnp.bfloat16),
        grid=(rows // tile,),
        in_specs=[block, pl.BlockSpec((1, model), lambda i: (0, 0))]
        + [pl.BlockSpec(memory_space=pl.ANY)] * len(also),
        out_specs=block,
        compiler_params=pltpu.CompilerParams(vmem_limit_bytes=VMEM_LIMIT),
        cost_estimate=SMALL,
        name="input_norm",
    )(hidden, gain.reshape(1, model), *also)


def project_kernel(index, *refs, count, final, has_acc, heads):
    xs, pieces, rest = refs[:count], refs[count : 2 * count], refs[2 * count :]
    x = jnp.concatenate([ref[...] for ref in xs], axis=1)
    weights = jnp.concatenate([ref[...] for ref in pieces], axis=0)
    total = jnp.dot(x, weights, preferred_element_type=jnp.float32)
    if has_acc:
        total = total + rest[0][...]
        rest = rest[1:]
    if not final:
        rest[0][...] = total
        return
    cos_ref, sin_ref, q_ref, k_ref, v_ref = rest
    cosine, sine = cos_ref[...], sin_ref[...]

    def rotate(u):
        return (u * cosine + pltpu.roll(u, HD // 2, 1) * sine).astype(jnp.bfloat16)

    for h in range(heads):
        q_ref[:, h * HD : (h + 1) * HD] = rotate(total[:, h * HD : (h + 1) * HD])
    key = total[:, heads * HD : (heads + 1) * HD]
    k_ref[...] = rotate(key.astype(jnp.bfloat16).astype(jnp.float32))
    v_ref[...] = total[:, (heads + 1) * HD :].astype(jnp.bfloat16)


def project(index, x, pieces, acc=None, rope=None, also=(), tile=256):
    rows, model = x.shape
    depth, width = pieces[0].shape
    count = len(pieces)
    heads = width // HD - 2
    final = rope is not None
    row_block = lambda w: pl.BlockSpec((tile, w), lambda i, *_: (i, 0))
    in_specs = [
        pl.BlockSpec((tile, depth), lambda i, at, k=k: (i, at[k])) for k in range(count)
    ] + [pl.BlockSpec((depth, width), lambda i, *_: (0, 0), pipeline_mode=pl.Buffered(1))] * count
    args = [x] * count + list(pieces)
    if acc is not None:
        in_specs.append(row_block(width))
        args.append(acc)
    if final:
        in_specs += [row_block(HD)] * 2
        args += list(rope)
        out_shape = [
            jax.ShapeDtypeStruct((rows, heads * HD), jnp.bfloat16),
            jax.ShapeDtypeStruct((rows, HD), jnp.bfloat16),
            jax.ShapeDtypeStruct((rows, HD), jnp.bfloat16),
        ]
        out_specs = [row_block(heads * HD), row_block(HD), row_block(HD)]
    else:
        out_shape = jax.ShapeDtypeStruct((rows, width), jnp.float32)
        out_specs = row_block(width)
    kernel = functools.partial(
        project_kernel, count=count, final=final, has_acc=acc is not None, heads=heads
    )
    kernel = skipping(kernel, 1 + len(args), len(also))
    in_specs += [pl.BlockSpec(memory_space=pl.ANY)] * len(also)
    args += list(also)
    return pl.pallas_call(
        kernel,
        out_shape=out_shape,
        grid_spec=pltpu.PrefetchScalarGridSpec(
            num_scalar_prefetch=1, grid=(rows // tile,), in_specs=in_specs, out_specs=out_specs
        ),
        compiler_params=pltpu.CompilerParams(vmem_limit_bytes=VMEM_LIMIT),
        cost_estimate=SMALL,
        name="project",
    )(index, *args)


def attend_kernel(
    scal, q_ref, k_ref, v_ref, c_ref, *rest, first, heads, tq, tk
):
    o_ref, m_ref, acc_ref = rest[-3:]
    base = first + pl.program_id(0) * tq
    rows = heads * tq
    q = jnp.concatenate([q_ref[:, h * HD : (h + 1) * HD] for h in range(heads)], axis=0)
    m_ref[...] = jnp.full((rows, HD), lowest_peak, jnp.float32)
    acc_ref[...] = jnp.zeros((rows, 2 * HD), jnp.float32)
    token = base + lax.broadcasted_iota(jnp.int32, (tq, 1), 0)
    scale = HD ** (-0.5) * 1.4426950408889634

    def update(keys, values, mask):
        width = keys.shape[0]
        s = lax.dot_general(q, keys, (((1,), (1,)), ((), ())), preferred_element_type=jnp.float32)
        s = s.reshape(heads, tq, width) * scale
        s = jnp.where(mask[None], s, masked_score).reshape(rows, width)
        before = m_ref[...]
        peak = jnp.maximum(before, jnp.max(s, axis=1, keepdims=True))
        m_ref[...] = peak
        keep = jnp.exp2(before - peak)
        p = jnp.exp2(s - jnp.concatenate([peak] * (width // HD), axis=1)).astype(jnp.bfloat16)
        wide = jnp.concatenate([values, jnp.ones((width, HD), jnp.bfloat16)], axis=1)
        acc_ref[...] = acc_ref[...] * jnp.concatenate([keep, keep], axis=1) + jnp.dot(
            p, wide, preferred_element_type=jnp.float32
        )

    for r in range(REQ_REP):
        start, end, pref = scal[r], scal[REQ_REP + r], scal[2 * REQ_REP + r]
        inside = (token >= start) & (token < end)

        @pl.when((start < base + tq) & (end > base))
        def _(r=r, start=start, end=end, pref=pref, inside=inside):
            @pl.loop(0, (pref + tk - 1) // tk)
            def _(j):
                at = pl.ds(pl.multiple_of(r * PREF_MAX + j * tk, tk), tk)
                slot = j * tk + lax.broadcasted_iota(jnp.int32, (1, tk), 1)
                update(c_ref[at, :HD], c_ref[at, HD:], inside & (slot < pref))

            @pl.loop(start // tk, (jnp.minimum(end, base + tq) - 1) // tk + 1)
            def _(j):
                at = pl.ds(pl.multiple_of(j * tk, tk), tk)
                other = j * tk + lax.broadcasted_iota(jnp.int32, (1, tk), 1)
                update(k_ref[at, :], v_ref[at, :], inside & (other >= start) & (other <= token))

    out = (acc_ref[:, :HD] / acc_ref[:, HD:]).astype(jnp.bfloat16)
    for h in range(heads):
        o_ref[:, h * HD : (h + 1) * HD] = out[h * tq : (h + 1) * tq]


def attend(scal, q, k, v, cache, first, rows, earlier=None, also=(), tq=128, tk=256):
    heads = q.shape[1] // HD
    tokens, slots = q.shape[0], cache.shape[0]
    whole = lambda r, w: pl.BlockSpec((r, w), lambda i, *_: (0, 0))
    block = pl.BlockSpec((tq, heads * HD), lambda i, *_: (first // tq + i, 0))
    more = ([] if earlier is None else [earlier]) + list(also)
    return pl.pallas_call(
        functools.partial(attend_kernel, first=first, heads=heads, tq=tq, tk=tk),
        out_shape=jax.ShapeDtypeStruct((tokens, heads * HD), jnp.bfloat16),
        grid_spec=pltpu.PrefetchScalarGridSpec(
            num_scalar_prefetch=1,
            grid=(rows // tq,),
            in_specs=[
                block,
                whole(tokens, HD),
                whole(tokens, HD),
                pl.BlockSpec((slots, 2 * HD), lambda i, s: (0, s[3 * REQ_REP])),
            ]
            + [pl.BlockSpec(memory_space=pl.ANY)] * len(more),
            out_specs=block,
            scratch_shapes=[
                pltpu.VMEM((heads * tq, HD), jnp.float32),
                pltpu.VMEM((heads * tq, 2 * HD), jnp.float32),
            ],
        ),
        input_output_aliases={} if earlier is None else {5: 0},
        compiler_params=pltpu.CompilerParams(vmem_limit_bytes=VMEM_LIMIT),
        cost_estimate=SMALL,
        name="attend",
    )(scal, q, k, v, cache, *more)


def output_kernel(choice, a_ref, *rest, count, slots):
    pieces, outs, (held, sems) = rest[:count], rest[count : count + slots], rest[count + slots :]
    width = outs[0].shape[1]

    @pl.when(pl.program_id(0) == 0)
    def _():
        for s in range(slots):
            for i in range(count):

                @pl.when(choice[s] == i)
                def _(s=s, i=i):
                    pltpu.make_async_copy(
                        pieces[i], held.at[:, pl.ds(s * width, width)], sems.at[s]
                    ).start()

        for s in range(slots):
            pltpu.make_async_copy(
                pieces[0], held.at[:, pl.ds(s * width, width)], sems.at[s]
            ).wait()

    part = jnp.dot(a_ref[...], held[...], preferred_element_type=jnp.float32)
    part = part.astype(jnp.bfloat16)
    for s in range(slots):
        outs[s][...] = part[:, s * width : (s + 1) * width]


def output_parts(choice, attended, pieces, slots, also=(), tile=512):
    rows, depth = attended.shape
    width = pieces[0].shape[1]
    count = len(pieces)
    kernel = functools.partial(output_kernel, count=count, slots=slots)
    return pl.pallas_call(
        skipping(kernel, 2 + count, len(also)),
        out_shape=[jax.ShapeDtypeStruct((rows, width), jnp.bfloat16)] * slots,
        grid_spec=pltpu.PrefetchScalarGridSpec(
            num_scalar_prefetch=1,
            grid=(rows // tile,),
            in_specs=[pl.BlockSpec((tile, depth), lambda i, *_: (i, 0))]
            + [pl.BlockSpec(memory_space=pl.ANY)] * (count + len(also)),
            out_specs=[pl.BlockSpec((tile, width), lambda i, *_: (i, 0))] * slots,
            scratch_shapes=[
                pltpu.VMEM((depth, slots * width), jnp.bfloat16),
                pltpu.SemaphoreType.DMA((slots,)),
            ],
        ),
        compiler_params=pltpu.CompilerParams(vmem_limit_bytes=VMEM_LIMIT),
        cost_estimate=SMALL,
        name="output_parts",
    )(choice, attended, *pieces, *also)


def residual_kernel(where, h_ref, *rest, stages, last):
    terms, rest = rest[: 3 * stages], rest[3 * stages :]
    r_ref, ssq_ref = rest[-2:]
    width = terms[0].shape[1]
    total = rest[1][...] if last else None
    for s in range(stages):
        at = slice(None) if last else pl.ds(pl.multiple_of(where[s] * width, width), width)
        proj = sum(term[...].astype(jnp.float32) for term in terms[3 * s : 3 * s + 3])
        resid = (h_ref[:, at].astype(jnp.float32) + proj).astype(jnp.bfloat16)
        r_ref[:, at] = resid
        wide = resid.astype(jnp.float32)
        square = wide * wide
        for i in range(0, width, HD):
            part = square[:, i : i + HD]
            total = part if total is None else total + part
    if last:
        total = lax.dot_general(
            jnp.ones((8, HD), jnp.float32),
            total,
            (((1,), (1,)), ((), ())),
            precision=lax.Precision.HIGHEST,
            preferred_element_type=jnp.float32,
        )
    ssq_ref[...] = total


def residual(where, hidden, terms, total_width, earlier=None, tile=512):
    rows = hidden.shape[0]
    stages = len(terms)
    terms = [term for stage in terms for term in stage]
    width = terms[0].shape[1]
    last = earlier is not None
    parts = [pl.BlockSpec((tile, width), lambda i, *_: (i, 0))] * len(terms)
    lanes = pl.BlockSpec((tile, HD), lambda i, *_: (i, 0))
    if last:
        in_place = pl.BlockSpec((tile, width), lambda i, w: (i, w[1]))
        out_place = pl.BlockSpec((tile, width), lambda i, w: (i, w[0]))
        more, more_specs = list(earlier), [pl.BlockSpec(memory_space=pl.ANY), lanes]
        aliases = {2 + len(terms): 0}
        ssq_shape, ssq_block = (8, rows), pl.BlockSpec((8, tile), lambda i, *_: (0, i))
    else:
        count = where.shape[0] - 1
        in_place = pl.BlockSpec((tile, total_width), lambda i, w: (i, w[count]))
        out_place = pl.BlockSpec((tile, total_width), lambda i, *_: (i, 0))
        more, more_specs, aliases = [], [], {}
        ssq_shape, ssq_block = (rows, HD), lanes
    return pl.pallas_call(
        functools.partial(residual_kernel, stages=stages, last=last),
        out_shape=[
            jax.ShapeDtypeStruct((rows, total_width), jnp.bfloat16),
            jax.ShapeDtypeStruct(ssq_shape, jnp.float32),
        ],
        grid_spec=pltpu.PrefetchScalarGridSpec(
            num_scalar_prefetch=1,
            grid=(rows // tile,),
            in_specs=[in_place] + parts + more_specs,
            out_specs=[out_place, ssq_block],
        ),
        input_output_aliases=aliases,
        compiler_params=pltpu.CompilerParams(vmem_limit_bytes=VMEM_LIMIT),
        cost_estimate=SMALL,
        name="residual",
    )(where, hidden, *terms, *more)


def output_norm_kernel(*refs, count, model):
    squares, (r_ref, gain_ref, out_ref) = refs[:count], refs[count:]
    total = lax.dot_general(
        jnp.concatenate([ref[...] for ref in squares], axis=0),
        jnp.ones((8 * count, HD), jnp.float32),
        (((0,), (0,)), ((), ())),
        precision=lax.Precision.HIGHEST,
        preferred_element_type=jnp.float32,
    )
    factor = lax.rsqrt(total * (1.0 / (8 * model)) + norm_eps)
    for i in range(0, r_ref.shape[1], HD):
        at = slice(i, i + HD)
        out_ref[:, at] = (r_ref[:, at].astype(jnp.float32) * factor * gain_ref[:, at]).astype(
            jnp.bfloat16
        )


def output_norm(squares, resid, gain, model, tile=512):
    rows, width = resid.shape
    block = pl.BlockSpec((tile, width), lambda i: (i, 0))
    return pl.pallas_call(
        functools.partial(output_norm_kernel, count=len(squares), model=model),
        out_shape=jax.ShapeDtypeStruct((rows, width), jnp.bfloat16),
        grid=(rows // tile,),
        in_specs=[pl.BlockSpec((8, tile), lambda i: (0, i))] * len(squares)
        + [block, pl.BlockSpec((1, width), lambda i: (0, 0))],
        out_specs=block,
        compiler_params=pltpu.CompilerParams(vmem_limit_bytes=VMEM_LIMIT),
        cost_estimate=SMALL,
        name="output_norm",
    )(*squares, resid, gain)


def join_kernel(*refs):
    pass


def join(arrays, *others):
    anywhere = pl.BlockSpec(memory_space=pltpu.HBM)
    count = len(arrays)
    return tuple(
        pl.pallas_call(
            join_kernel,
            out_shape=[jax.ShapeDtypeStruct(p.shape, p.dtype) for p in arrays],
            in_specs=[anywhere] * count + [pl.BlockSpec(memory_space=pl.ANY)] * len(others),
            out_specs=[anywhere] * count,
            input_output_aliases={i: i for i in range(count)},
            compiler_params=pltpu.CompilerParams(vmem_limit_bytes=VMEM_LIMIT),
            cost_estimate=SMALL,
            name="join",
        )(*arrays, *others)
    )


def body(hidden, norm_gain, w_query, w_keyval, w_output, cache, lengths, prefix, out_gain):
    n_rep, n_tp = lax.axis_size("rep"), lax.axis_size("tp")
    rep, tp = lax.axis_index("rep"), lax.axis_index("tp")
    rows, model = hidden.shape
    heads_here = w_query.shape[1] // HD
    order, source, piece, column, last = tables(n_rep, n_tp)
    ahead = [(order[i], order[(i + 1) % n_rep]) for i in range(n_rep)]
    back = [(b, a) for a, b in ahead]
    swap = lambda value, d: lax.ppermute(value, "tp", [(i, i ^ d) for i in range(n_tp)])
    step = lambda pair: (lax.ppermute(pair[0], "rep", ahead), lax.ppermute(pair[1], "rep", back))

    mid = w_output.shape[1] // 2
    out_pairs = [(w_output[:, :mid], w_output[:, mid:])]
    out_pairs.append(step(out_pairs[0]))

    kv_head_of = lambda t: t * heads_here // (H // KV)
    feats = w_keyval.shape[1] // KV
    col = jnp.arange(w_keyval.shape[1], dtype=jnp.int32)[:, None]
    feat = jnp.arange(feats, dtype=jnp.int32)[None, :]
    parts = []
    for d in range(n_tp):
        pick = (col == feat * KV + kv_head_of(tp ^ d)).astype(jnp.bfloat16)
        mine = jnp.dot(w_keyval, pick, preferred_element_type=jnp.float32).astype(jnp.bfloat16)
        parts.append(swap(mine, d) if d else mine)
    mixed = jnp.concatenate(parts, axis=1)
    slot = jnp.arange(mixed.shape[1], dtype=jnp.int32)
    home = ((slot // feats) ^ tp) * feats + slot % feats
    place = (home[:, None] == slot[None, :]).astype(jnp.bfloat16)
    keyval = jnp.dot(mixed, place, preferred_element_type=jnp.float32).astype(jnp.bfloat16)

    joined = jnp.concatenate([w_query, keyval], axis=1)
    depth = joined.shape[0] // 2

    lens = lengths.reshape(-1)
    position, starts, ends = request_position(lens, prefix, rows)
    rope = rope_tables(position)
    scal = jnp.concatenate(
        [starts, ends, prefix, kv_head_of(tp).astype(jnp.int32)[None]]
    ).astype(jnp.int32)

    bits = n_tp.bit_length() - 1
    dests = tp ^ jnp.asarray([bit_reverse(s, bits) for s in range(n_tp)], jnp.int32)
    choice_all = jnp.asarray(piece)[rep][dests]
    column_all = jnp.asarray(column)[rep][tp]
    halves = piece.shape[2]
    choices = [choice_all[:, s] for s in range(halves)]
    where_early = jnp.concatenate([column_all[:-1], tp[None]]).astype(jnp.int32)
    where_last = jnp.stack([column_all[-1], tp * halves + column_all[-1]]).astype(jnp.int32)
    width = model // n_tp
    gain = lax.dynamic_slice_in_dim(out_gain, tp * width, width, 0).astype(jnp.float32).reshape(1, width)

    first_cut, second_cut = n_rep // 2, n_rep - 2
    index = jnp.asarray(source)[rep]
    cuts = [0, first_cut, second_cut, n_rep]
    indices = [index[2 * low : 2 * high] for low, high in zip(cuts[:-1], cuts[1:])]
    in_pairs = [join((joined[:depth], joined[depth:]), *out_pairs[1])]
    x = input_norm(hidden, norm_gain, in_pairs[0][:1])
    acc, done = None, 0

    def project_arrived(acc, done, rope=None, also=()):
        ready = [p for pair in in_pairs[done:] for p in pair]
        return project(indices[cuts.index(done)], x, ready, acc, rope, also)

    for k in range(1, n_rep):
        arrived = step(in_pairs[-1])
        if k == 2:
            arrived = join(arrived, x)
        if k == 3:
            arrived = join(
                arrived, scal, *rope, *choices, where_early, where_last, gain, *indices
            )
        if k in (first_cut, second_cut):
            acc, done = project_arrived(acc, done), k
            arrived = join(arrived, acc)
        in_pairs.append(arrived)

    out_pairs[1] = join(out_pairs[1], *in_pairs[-1])
    q, k, v = project_arrived(acc, done, rope, out_pairs[1][:1])

    def stage(members, attended, also=()):
        pieces = [p for pair in out_pairs[: last[members[-1]] + 1] for p in pair]
        choice = jnp.stack([choices[s] for s in members], axis=1).reshape(-1)
        return output_parts(choice, attended, pieces, choice.shape[0], also)

    def exchange(parts, count):
        d = 1
        while True:
            half = len(parts) // 2
            received = [swap(part, d) for part in parts[half:]]
            pairs = list(zip(parts[:half], received))
            if half == 2 * count:
                return pairs[:count], pairs[count:]
            parts, d = [add(*pair) for pair in pairs], d * 2

    def add(a, b):
        return (a.astype(jnp.float32) + b.astype(jnp.float32)).astype(jnp.bfloat16)

    terms = []

    def collect(parts, cut=None):
        spans = [slice(0, rows)] if cut is None else [slice(0, cut), slice(cut, rows)]
        all_sends, all_recvs = [], []
        for stay, leave in zip(*exchange(parts, len(parts) // n_tp)):
            sends = [add(*(a[span] for a in leave)) for span in spans]
            recvs = [swap(part, n_tp // 2) for part in sends]
            terms.append((*stay, recvs[0] if cut is None else jnp.concatenate(recvs, axis=0)))
            all_sends += sends
            all_recvs += recvs
        return all_sends, all_recvs

    shares = [0, 4, 8]
    tq = rows // shares[-1]
    attended, raw, sent, pending = None, None, [], [[s] for s in range(halves)]
    if halves > 3:
        pending[:2] = [[0, 1]]
    for flight in range(2, n_rep):
        arrived = step(out_pairs[-1])
        own = list(out_pairs[-1][:1])
        waits = []
        if flight == 2:
            waits = [q]
        elif flight - 3 < len(shares) - 1:
            low, high = shares[flight - 3 : flight - 1]
            attended = attend(
                scal, q, k, v, cache, low * tq, (high - low) * tq, attended, own, tq=tq
            )
            waits = [attended]
        if flight > len(shares) + 1:
            gates = [*own, *sent[:1]]
            waits += sent[1:]
            sent = []
            if raw is not None:
                sends, sent = collect(raw)
                waits, raw = waits + sends, None
            elif last[pending[0][-1]] < flight and len(pending) > 1:
                raw = stage(pending.pop(0), attended, gates)
                half = len(raw) // 2
                arrived = join((*arrived, *raw[half:]), *waits)
                raw, arrived, waits = [*raw[:half], *arrived[2:]], arrived[:2], []
        out_pairs.append(join(arrived, *waits) if waits else tuple(arrived))

    recvs = []
    while pending:
        gates = []
        if raw is not None:
            gates, recvs = collect(raw, rows * 3 // 4)
        raw = stage(pending.pop(0), attended, gates)
    early = residual(where_early, hidden, terms, width)
    half = len(raw) // 2
    raw = [*raw[:half], *join(raw[half:], *recvs[:1])]
    collect(raw)
    resid, ssq = residual(where_last, hidden, terms[-1:], width, early)

    squares = [ssq] + [swap(ssq, d) for d in range(1, n_tp)]
    normed = output_norm(squares, resid, gain, model)
    return (resid, normed)


def solution(mesh):
    placed = (
        P("rep", None),
        P(),
        P("rep", "tp"),
        P("rep", "tp"),
        P("tp", "rep"),
        P("rep", None),
        P("rep", None),
        P("rep"),
        P(),
    )
    return jax.shard_map(
        body,
        mesh=mesh,
        in_specs=placed,
        out_specs=(P("rep", "tp"), P("rep", "tp")),
        check_vma=False,
    )
```
